256 devices in a mesh: node: 32 (over x, z), local: 8 (over y, core).
Axes of the slice: x: 4, y: 4, z: 8, core: 2. Of those that a mesh axis runs over, the one named last changes fastest.
Arguments:
- tokens_in: bfloat16 [4096, 4096], P('node', 'local'), may hold values from -6 to 6
- grad_out: bfloat16 [4096, 4096], P('node', 'local'), may hold values from -6 to 6
- expert_ids: int32 [4096, 4], P('node'), may hold values from 0 to 31, all different within a row; in each aligned block of 128 rows (0 to 127, 128 to 255, ...) at most 24 rows name the same one
- w_gate: bfloat16 [32, 4096, 2048], P('node', None, 'local'), may hold values from -0.09375 to 0.09375
- w_up: bfloat16 [32, 4096, 2048], P('node', None, 'local'), may hold values from -0.09375 to 0.09375
- w_down: bfloat16 [32, 2048, 4096], P('node', 'local'), may hold values from -0.125 to 0.125
Outputs:
- grad_in: bfloat16 [4096, 4096], P('node', 'local')
- grad_gate: bfloat16 [32, 4096, 2048], P('node', None, 'local')
- grad_up: bfloat16 [32, 4096, 2048], P('node', None, 'local')
- grad_down: bfloat16 [32, 2048, 4096], P('node', 'local')
The draws below stay inside these ranges and needn't reach their ends.
Inputs may be any that keep to these rules, and one draw needn't show every extreme that they name: `expert_ids`: each token names 4 different experts; within the tokens of one index of node (aligned blocks of 128 tokens) an expert is named by at most 24 tokens, a bound that some block reaches.
All inputs are finite; a program needn't handle non-finite values.
Results may differ from the reference program's by a relative error of at most 0.019.
Values may be sent and summed in bfloat16 or wider, within the bound.
No kernel may reach another device: no remote copies, remote signals or barrier semaphores. Data moves between devices by JAX's collectives and lax.ppermute only.
A program may use at most 128 MiB of HBM per device.

```python
import math
import jax
import jax.numpy as jnp
import numpy as np
from jax import lax

D = 4096
FF = 2048
TOPK = 4
TOK_NODE = 128
EXPERTS = 32
TOKENS = 4096
CAP = 24
N_NODE = 32
N_LOCAL = 8


def shard_levels(key, shape, split, least, high):
    def one(dim, blocks):
        heights = jax.random.uniform(jax.random.fold_in(jax.random.fold_in(key, 6), dim), (blocks,), jnp.float32, least / len(split), high / len(split))
        return jnp.repeat(jnp.exp(heights), shape[dim] // blocks).reshape((-1,) + (1,) * (len(shape) - dim - 1))

    level = one(*split[0])
    for cut in split[1:]:
        level = level * one(*cut)
    return level


def routed_block(rng, own, number, rows, amount, top, bound, lean):
    sequence = jax.random.permutation(rng, amount)
    crowded, common = load_shares(amount, rows * top, bound, lean, True), load_shares(amount, rows * top, bound, lean, False)
    places = jnp.arange(amount)

    def named(tallies, turn):
        used = int((tallies > 0).sum())
        fixed = max(1, used // 4)
        moved = fixed + (places - fixed + turn * (used - fixed)) % max(1, amount - fixed)
        return jnp.zeros((amount,), jnp.int32).at[sequence[jnp.where(places < fixed, places, moved)]].set(jnp.asarray(tallies, jnp.int32))

    tallies = jnp.where(number % 4 == 0, named(crowded, number // 4), named(common, number - number // 4 - 1))
    mixed = jax.random.permutation(jax.random.fold_in(own, 3), amount)
    source_of, sink = mixed[0:amount // 2 * 2:2], mixed[1:amount // 2 * 2:2]
    room = jnp.minimum(tallies[source_of] - 1, bound - tallies[sink]) // 2
    room = jnp.where((source_of == sequence[0]) | (sink == sequence[0]) | (tallies[sink] == 0), 0, jnp.maximum(room, 0))
    moved = jax.random.randint(jax.random.fold_in(own, 4), (amount // 2,), 0, 1 << 20) % (room + 1)
    tallies = tallies.at[source_of].add(-moved).at[sink].add(moved)
    labels = jnp.searchsorted(jnp.cumsum(tallies), jnp.arange(rows * top), side="right").astype(jnp.int32)
    table = labels.reshape(top, rows).T
    table = table[jax.random.permutation(jax.random.fold_in(own, 1), rows)]
    turn = jax.random.randint(jax.random.fold_in(own, 2), (rows, 1), 0, top)
    return jnp.take_along_axis(table, (jnp.arange(top)[None, :] + turn) % top, axis=1)


def load_shares(count, total, reach, slope, full):
    weights = [(1 << 20) // math.isqrt(standing ** slope) + 1 for standing in range(1, count + 1)]
    largest = reach if full else min(reach, max(-(-total // count), total * weights[0] // sum(weights)))
    least = 1 if total - largest >= count - 1 else 0
    counts, surplus = [largest] + [least] * (count - 1), total - largest - least * (count - 1)
    while surplus > 0:
        free = [i for i in range(1, count) if counts[i] < largest] or [i for i in range(1, count) if counts[i] < reach]
        pool, remaining = sum([weights[i] for i in free]), surplus
        for i in free:
            more = min(reach - counts[i], max(1, remaining * weights[i] // pool), surplus)
            counts[i] = counts[i] + more
            surplus = surplus - more
    return np.array(counts)


def noise(rng, extent, deviation, bound, cuts=(), kind=jnp.bfloat16):
    entries = jax.random.normal(rng, extent, jnp.float32) * deviation
    if len(cuts) > 0:
        entries = shard_levels(rng, extent, cuts, -0.22, 0.18) * entries
    return jnp.clip(entries, min=-bound, max=bound).astype(kind)


def setup_inputs(seed: int = 0) -> dict:
    splits = jax.random.split(jax.random.key(seed), 7)
    tokens_in = noise(splits[0], (TOKENS, D), 1.0, 6.0, ((0, 32), (1, 8)))
    grad_out = noise(splits[1], (TOKENS, D), 1.0, 6.0, ((0, 32), (1, 8)))
    expert_ids_keys = jax.random.split(jax.random.fold_in(splits[2], 1), TOKENS // TOK_NODE)
    expert_ids_turns = jax.random.permutation(jax.random.fold_in(splits[2], 3), TOKENS // TOK_NODE)
    expert_ids = jax.vmap(lambda own, number: routed_block(jax.random.fold_in(splits[2], 2), own, number, TOK_NODE, EXPERTS, TOPK, CAP, 2))(expert_ids_keys, expert_ids_turns).reshape((TOKENS, TOPK))
    w_gate = noise(splits[3], (EXPERTS, D, FF), D ** -0.5, 0.09375, ((0, 32), (2, 8)))
    w_up = noise(splits[4], (EXPERTS, D, FF), D ** -0.5, 0.09375, ((0, 32), (2, 8)))
    w_down = noise(splits[5], (EXPERTS, FF, D), FF ** -0.5, 0.125, ((0, 32), (1, 8)))
    return {"tokens_in": tokens_in, "grad_out": grad_out, "expert_ids": expert_ids, "w_gate": w_gate, "w_up": w_up, "w_down": w_down}


def route_slots(block_ids, experts, capacity):
    flattened = block_ids.reshape(-1)
    matches = (flattened[:, None] == jnp.arange(experts, dtype=jnp.int32)[None, :]).astype(jnp.int32)
    earlier = jnp.cumsum(matches, axis=0) - matches
    position = jnp.sum(earlier * matches, axis=1)
    return (flattened * capacity + position).astype(jnp.int32)


def slot_owners(slot_index, experts, capacity, topk):
    token_index = (jnp.arange(slot_index.shape[0], dtype=jnp.int32) // topk).astype(jnp.int32)
    owners = jnp.zeros((experts * capacity,), jnp.int32).at[slot_index].set(token_index)
    filled = jnp.zeros((experts * capacity,), jnp.int32).at[slot_index].set(1)
    return owners, filled


def pack_rows(row_table, owners, filled):
    picked = row_table[owners]
    return jnp.where(filled[:, None] > 0, picked, jnp.zeros_like(picked))


def expert_step(operands):
    rows_in, rows_grad, gate_w, up_w, down_w = operands
    gate_pre = jnp.dot(rows_in, gate_w, preferred_element_type=jnp.float32)
    up_pre = jnp.dot(rows_in, up_w, preferred_element_type=jnp.float32)
    hidden_grad = jnp.dot(rows_grad, down_w.T, preferred_element_type=jnp.float32)
    sigmoid_gate = jax.nn.sigmoid(gate_pre)
    swish_gate = gate_pre * sigmoid_gate
    active = (swish_gate * up_pre).astype(jnp.bfloat16)
    gate_grad = (hidden_grad * up_pre * sigmoid_gate * (1.0 + gate_pre * (1.0 - sigmoid_gate))).astype(jnp.bfloat16)
    up_grad = (hidden_grad * swish_gate).astype(jnp.bfloat16)
    down_total = jnp.dot(active.T, rows_grad, preferred_element_type=jnp.float32).astype(jnp.bfloat16)
    gate_total = jnp.dot(rows_in.T, gate_grad, preferred_element_type=jnp.float32).astype(jnp.bfloat16)
    up_total = jnp.dot(rows_in.T, up_grad, preferred_element_type=jnp.float32).astype(jnp.bfloat16)
    row_count = rows_in.shape[0]
    block_width = FF // N_LOCAL
    partial_value = jnp.einsum("rlf,dlf->rld",
                         gate_grad.astype(jnp.float32).reshape(row_count, N_LOCAL, block_width),
                         gate_w.astype(jnp.float32).reshape(D, N_LOCAL, block_width))
    partial_value = partial_value + jnp.einsum("rlf,dlf->rld",
                                   up_grad.astype(jnp.float32).reshape(row_count, N_LOCAL, block_width),
                                   up_w.astype(jnp.float32).reshape(D, N_LOCAL, block_width))
    rounded = lax.optimization_barrier(partial_value.astype(jnp.bfloat16)).astype(jnp.float32)
    return jnp.sum(rounded, axis=1), gate_total, up_total, down_total


def reference(tokens_in, grad_out, expert_ids, w_gate, w_up, w_down):
    node_ids = expert_ids.reshape(N_NODE, TOK_NODE, TOPK)
    slot_index = jax.vmap(lambda node_block: route_slots(node_block, EXPERTS, CAP))(node_ids)
    owners, filled = jax.vmap(lambda slot_row: slot_owners(slot_row, EXPERTS, CAP, TOPK))(slot_index)

    def gather_rows(array_in):
        blocks = array_in.reshape(N_NODE, TOK_NODE, D)
        packed = jax.vmap(pack_rows)(blocks, owners, filled)
        return packed.reshape(N_NODE, EXPERTS, CAP, D).transpose(1, 0, 2, 3).reshape(EXPERTS, N_NODE * CAP, D)

    returned, grad_gate, grad_up, grad_down = lax.map(
        expert_step, (gather_rows(tokens_in), gather_rows(grad_out), w_gate, w_up, w_down))
    returned_rows = returned.reshape(EXPERTS, N_NODE, CAP, D).transpose(1, 0, 2, 3).reshape(N_NODE, EXPERTS * CAP, D)
    picked = jax.vmap(lambda row_table, slot_row: row_table[slot_row])(returned_rows, slot_index)
    grad_in = jnp.sum(picked.reshape(N_NODE, TOK_NODE, TOPK, D), axis=2).reshape(TOKENS, D).astype(jnp.bfloat16)
    return grad_in, grad_gate, grad_up, grad_down
```

```python
import jax
import jax.numpy as jnp
from jax import lax
from jax.sharding import PartitionSpec as P


def slot_onehot(block_ids, experts, capacity):
    tokens = block_ids.shape[0]
    named = jnp.sum(
        (block_ids[:, :, None] == jnp.arange(experts, dtype=jnp.int32)).astype(jnp.bfloat16), axis=1
    )
    row = lax.broadcasted_iota(jnp.int32, (tokens, tokens), 0)
    column = lax.broadcasted_iota(jnp.int32, (tokens, tokens), 1)
    before = (column < row).astype(jnp.bfloat16)
    earlier = jnp.einsum("se,ts->et", named, before, preferred_element_type=jnp.float32)
    place = jnp.where(named.T > 0, earlier.astype(jnp.int32), -1)
    slot = jnp.arange(capacity, dtype=jnp.int32)
    onehot = (place[:, None, :] == slot[None, :, None]).astype(jnp.bfloat16)
    return onehot.reshape(experts * capacity, tokens)


def body(tokens_in, grad_out, expert_ids, w_gate, w_up, w_down):
    experts = lax.axis_size("node")
    token_count, topk = expert_ids.shape
    capacity = token_count * topk * 3 // (2 * experts)
    onehot = slot_onehot(expert_ids, experts, capacity)

    def rows_of(table):
        packed = jnp.dot(onehot, table, preferred_element_type=jnp.float32).astype(jnp.bfloat16)
        arrived = lax.all_to_all(packed, "node", split_axis=0, concat_axis=0, tiled=True)
        return lax.all_gather(arrived, "local", axis=1, tiled=True)

    rows_in = rows_of(tokens_in)
    rows_grad = rows_of(grad_out)
    gate_w, up_w, down_w = w_gate[0], w_up[0], w_down[0]
    gate_pre = jnp.dot(rows_in, gate_w, preferred_element_type=jnp.float32)
    up_pre = jnp.dot(rows_in, up_w, preferred_element_type=jnp.float32)
    hidden_grad = jnp.einsum("rd,fd->rf", rows_grad, down_w, preferred_element_type=jnp.float32)
    sigmoid_gate = jax.nn.sigmoid(gate_pre)
    swish_gate = gate_pre * sigmoid_gate
    active = (swish_gate * up_pre).astype(jnp.bfloat16)
    gate_grad = (
        hidden_grad * up_pre * sigmoid_gate * (1.0 + gate_pre * (1.0 - sigmoid_gate))
    ).astype(jnp.bfloat16)
    up_grad = (hidden_grad * swish_gate).astype(jnp.bfloat16)
    partial_value = jnp.einsum("rf,df->rd", gate_grad, gate_w, preferred_element_type=jnp.float32)
    partial_value = partial_value + jnp.einsum(
        "rf,df->rd", up_grad, up_w, preferred_element_type=jnp.float32
    )
    summed = lax.psum_scatter(
        partial_value.astype(jnp.bfloat16), "local", scatter_dimension=1, tiled=True
    )
    returned = lax.all_to_all(summed, "node", split_axis=0, concat_axis=0, tiled=True)
    down_total = jnp.einsum("rf,rd->fd", active, rows_grad, preferred_element_type=jnp.float32)
    gate_total = jnp.einsum("rd,rf->df", rows_in, gate_grad, preferred_element_type=jnp.float32)
    up_total = jnp.einsum("rd,rf->df", rows_in, up_grad, preferred_element_type=jnp.float32)
    grad_in = jnp.einsum("st,sd->td", onehot, returned, preferred_element_type=jnp.float32)
    narrow = jnp.bfloat16
    return (
        grad_in.astype(narrow),
        gate_total.astype(narrow)[None],
        up_total.astype(narrow)[None],
        down_total.astype(narrow)[None],
    )


def solution(mesh):
    placed = (
        P("node", "local"),
        P("node", "local"),
        P("node", None),
        P("node", None, "local"),
        P("node", None, "local"),
        P("node", "local", None),
    )
    return jax.shard_map(
        body,
        mesh=mesh,
        in_specs=placed,
        out_specs=(
            P("node", "local"),
            P("node", None, "local"),
            P("node", None, "local"),
            P("node", "local", None),
        ),
        check_vma=False,
    )
```

```python
import functools

import jax
import jax.numpy as jnp
from jax import lax
from jax.experimental import pallas as pl
from jax.experimental.pallas import tpu as pltpu
from jax.sharding import PartitionSpec as P

F32 = jnp.float32
BF16 = jnp.bfloat16
HBM = pl.BlockSpec(memory_space=pltpu.HBM)
SMEM = pl.BlockSpec(memory_space=pltpu.SMEM)
VMEM = pl.BlockSpec(memory_space=pltpu.VMEM)
MIB = 1024 * 1024


def slot_places(block_ids, experts):
    tokens = block_ids.shape[0]
    named = jnp.sum(
        (block_ids[:, :, None] == jnp.arange(experts, dtype=jnp.int32)).astype(BF16), axis=1
    )
    row = lax.broadcasted_iota(jnp.int32, (tokens, tokens), 0)
    column = lax.broadcasted_iota(jnp.int32, (tokens, tokens), 1)
    before = (column < row).astype(BF16)
    earlier = jnp.einsum("se,ts->et", named, before, preferred_element_type=F32)
    return jnp.where(named.T > 0, earlier.astype(jnp.int32), -1)


def slot_onehot(places, first, count):
    experts, tokens = places.shape
    slot = first + jnp.arange(count, dtype=jnp.int32)
    onehot = (places[:, None, :] == slot[None, :, None]).astype(BF16)
    return onehot.reshape(experts * count, tokens)


def chip_step(value, step):
    size = lax.axis_size("local")
    chips = size // 2
    pairs = []
    for y in range(chips):
        pairs.append((2 * y, 2 * ((y + step) % chips)))
        pairs.append((2 * y + 1, 2 * ((y - step) % chips) + 1))
    return lax.ppermute(value, "local", pairs)


def core_swap(value):
    return lax.ppermute(value, "local", [(i, i ^ 1) for i in range(lax.axis_size("local"))])


def pin(values):
    return [pltpu.with_memory_space_constraint(value, pltpu.HBM) for value in values]


def after(value, *others):
    return lax.optimization_barrier((value, *others))[0]


def ring_gather(own, beside=()):
    back = chip_step(own, 1)
    on = chip_step(own, -1)
    sibling = core_swap(own)
    far = chip_step(after(back, *beside), 1)
    return (own, sibling, back, core_swap(back), on, core_swap(on)), far


def ring_order():
    size = lax.axis_size("local")
    chips = size // 2
    me = lax.axis_index("local")
    chip, core = me // 2, me % 2
    blocks = []
    for step in (0, -1, 1, 2):
        for other in (0, 1):
            from_core = (core + other) % 2
            moved = step * (1 - 2 * from_core)
            blocks.append(2 * ((chip + moved + chips) % chips) + from_core)
    return jnp.stack(blocks).astype(jnp.int32)


def piece_copies(pieces, buffer, sem):
    return [pltpu.make_async_copy(pieces[j], buffer.at[j], sem.at[j]) for j in range(8)]


def wait_for(ref, sem):
    pltpu.make_async_copy(ref, ref, sem).wait()


def finish(outs, sem):
    def step(j, carry):
        wait_for(outs.at[j], sem.at[j])
        return carry

    lax.fori_loop(0, outs.shape[0], step, 0)


def cost(rows, depth, columns, moved):
    return pl.CostEstimate(
        flops=2 * rows * depth * columns, bytes_accessed=moved, transcendentals=0
    )


def params(mib):
    return pltpu.CompilerParams(vmem_limit_bytes=mib * MIB)


def prepare_kernel(order, gate_a, gate_b, up_a, up_b, down_a, down_b, w_gu, own_t, send_t, w_dn):
    del order
    hidden = gate_a.shape[1]
    for i, (gate, up, down, turned) in enumerate(
        ((gate_a, up_a, down_a, own_t), (gate_b, up_b, down_b, send_t))
    ):
        w_gu[i, :, :hidden] = gate[...]
        w_gu[i, :, hidden:] = up[...]
        turned[0, :hidden, :] = gate[...].T
        turned[0, hidden:, :] = up[...].T
        w_dn[i] = down[...].T


def prepare_call(order, w_gate, w_up, w_down):
    depth, hidden = w_gate.shape
    width = depth // 8

    def rows(core):
        return pl.BlockSpec((width, hidden), lambda d, order: (order[2 * d + core], 0))

    def columns(core):
        return pl.BlockSpec((hidden, width), lambda d, order: (0, order[2 * d + core]))

    def out(count, *shape):
        return pl.BlockSpec((count, *shape), lambda d, order: (d, 0, 0))

    turned = pltpu.HBM((4, 2 * hidden, width), BF16)
    return pl.pallas_call(
        prepare_kernel,
        out_shape=(
            pltpu.HBM((8, width, 2 * hidden), BF16),
            turned,
            turned,
            pltpu.HBM((8, width, hidden), BF16),
        ),
        grid_spec=pltpu.PrefetchScalarGridSpec(
            num_scalar_prefetch=1,
            grid=(4,),
            in_specs=[rows(0), rows(1), rows(0), rows(1), columns(0), columns(1)],
            out_specs=(
                out(2, width, 2 * hidden),
                out(1, 2 * hidden, width),
                out(1, 2 * hidden, width),
                out(2, width, hidden),
            ),
        ),
        compiler_params=params(14),
        cost_estimate=cost(depth, hidden, 768, depth * hidden * 16),
        name="prepare",
    )(order, *pin((w_gate, w_gate, w_up, w_up, w_down, w_down)))


def gate_up_kernel(*refs):
    pieces, weights = refs[:8], refs[8]
    active, swish, slope, rows_in, w_gu, acc, row_sem, w_sem = refs[9:]
    hidden = active.shape[1]
    for j in range(8):
        pltpu.make_async_copy(weights.at[j], w_gu.at[j], w_sem.at[j]).start()
    for copy in piece_copies(pieces, rows_in, row_sem):
        copy.start()
    acc[...] = jnp.zeros_like(acc)

    def step(j, carry):
        wait_for(w_gu.at[j], w_sem.at[j])
        wait_for(rows_in.at[j], row_sem.at[j])
        acc[...] += jnp.dot(rows_in[j], w_gu[j], preferred_element_type=F32)
        return carry

    lax.fori_loop(0, 8, step, 0)
    gate_pre = acc[:, :hidden]
    up_pre = acc[:, hidden:]
    sigmoid_gate = jax.nn.sigmoid(gate_pre)
    swish_gate = gate_pre * sigmoid_gate
    swish[...] = swish_gate
    active[...] = (swish_gate * up_pre).astype(BF16)
    slope[...] = up_pre * sigmoid_gate * (1.0 + gate_pre * (1.0 - sigmoid_gate))


def gate_up_call(pieces, w_gu):
    rows, width = pieces[0].shape
    both = w_gu.shape[2]
    hidden = both // 2
    dma = pltpu.SemaphoreType.DMA((8,))
    return pl.pallas_call(
        gate_up_kernel,
        out_shape=(
            jax.ShapeDtypeStruct((rows, hidden), BF16),
            jax.ShapeDtypeStruct((rows, hidden), F32),
            jax.ShapeDtypeStruct((rows, hidden), F32),
        ),
        in_specs=[HBM] * 9,
        out_specs=(VMEM, VMEM, VMEM),
        scratch_shapes=[
            pltpu.VMEM((8, rows, width), BF16),
            pltpu.VMEM((8, width, both), BF16),
            pltpu.VMEM((rows, both), F32),
            dma,
            dma,
        ],
        compiler_params=params(16),
        cost_estimate=cost(rows, 8 * width, both, 8 * width * (rows + both) * 2),
        name="gate_up",
    )(*pin((*pieces, w_gu)))


def hidden_kernel(first, count, *refs):
    pieces, weights, before = refs[:count], refs[count], refs[count + 1]
    total, rows_grad, w_dn, row_sem, w_sem = refs[count + 2 :]
    for j in range(count):
        pltpu.make_async_copy(weights.at[first + j], w_dn.at[j], w_sem.at[j]).start()
        pltpu.make_async_copy(pieces[j], rows_grad.at[j], row_sem.at[j]).start()
    total[...] = jnp.zeros_like(total) if before is None else before[...]

    def step(j, carry):
        wait_for(w_dn.at[j], w_sem.at[j])
        wait_for(rows_grad.at[j], row_sem.at[j])
        total[...] += jnp.dot(rows_grad[j], w_dn[j], preferred_element_type=F32)
        return carry

    lax.fori_loop(0, count, step, 0)


def hidden_start_kernel(count, *refs):
    hidden_kernel(0, count, *refs[: count + 1], None, *refs[count + 1 :])


def hidden_end_kernel(first, count, *refs):
    before, swish, slope, grads, rows_grad, w_dn, acc, row_sem, w_sem = refs[count + 1 :]
    hidden_kernel(
        first, count, *refs[: count + 1], before, acc, rows_grad, w_dn, row_sem, w_sem
    )
    hidden = acc.shape[1]
    hidden_grad = acc[...]
    grads[:, :hidden] = (hidden_grad * slope[...]).astype(BF16)
    grads[:, hidden:] = (hidden_grad * swish[...]).astype(BF16)


def hidden_scratch(count, rows, width, hidden):
    dma = pltpu.SemaphoreType.DMA((count,))
    return [pltpu.VMEM((count, rows, width), BF16), pltpu.VMEM((count, width, hidden), BF16)], [
        dma,
        dma,
    ]


def hidden_start_call(pieces, w_dn):
    rows, width = pieces[0].shape
    hidden, count = w_dn.shape[2], len(pieces)
    buffers, sems = hidden_scratch(count, rows, width, hidden)
    return pl.pallas_call(
        functools.partial(hidden_start_kernel, count),
        out_shape=jax.ShapeDtypeStruct((rows, hidden), F32),
        in_specs=[HBM] * (count + 1),
        out_specs=VMEM,
        scratch_shapes=buffers + sems,
        compiler_params=params(15),
        cost_estimate=cost(rows, count * width, hidden, count * width * (rows + hidden) * 2),
        name="hidden_start",
    )(*pin((*pieces, w_dn)))


def hidden_end_call(pieces, w_dn, before, swish, slope):
    rows, width = pieces[0].shape
    hidden, count = w_dn.shape[2], len(pieces)
    buffers, sems = hidden_scratch(count, rows, width, hidden)
    return pl.pallas_call(
        functools.partial(hidden_end_kernel, w_dn.shape[0] - count, count),
        out_shape=jax.ShapeDtypeStruct((rows, 2 * hidden), BF16),
        in_specs=[HBM] * (count + 1) + [VMEM] * 3,
        out_specs=VMEM,
        scratch_shapes=buffers + [pltpu.VMEM((rows, hidden), F32)] + sems,
        compiler_params=params(12),
        cost_estimate=cost(rows, count * width, hidden, count * width * (rows + hidden) * 2),
        name="hidden_end",
    )(*pin((*pieces, w_dn)), before, swish, slope)


def partial_kernel(blocks, *refs):
    count = len(blocks)
    grads, other, own_w, other_w = refs[:4]
    outs = refs[4 : 4 + count]
    own_buf, other_buf, result, own_sem, other_sem, out_sem = refs[4 + count :]
    for i, j in enumerate(blocks):
        pltpu.make_async_copy(own_w.at[j], own_buf.at[i], own_sem.at[i]).start()
        pltpu.make_async_copy(other_w.at[j], other_buf.at[i], other_sem.at[i]).start()
    for i in range(count):
        wait_for(own_buf.at[i], own_sem.at[i])
        total = jnp.dot(grads[...], own_buf[i], preferred_element_type=F32)
        wait_for(other_buf.at[i], other_sem.at[i])
        total = total + jnp.dot(other[...], other_buf[i], preferred_element_type=F32)
        result[i] = total.astype(BF16)
        pltpu.make_async_copy(result.at[i], outs[i], out_sem.at[i]).start()
    finish(result, out_sem)


def partial_call(grads, other, own_w, other_w, blocks):
    both, width = own_w.shape[1:]
    rows, count = grads.shape[0], len(blocks)
    dma = pltpu.SemaphoreType.DMA((count,))
    return pl.pallas_call(
        functools.partial(partial_kernel, blocks),
        out_shape=[pltpu.HBM((rows, width), BF16)] * count,
        in_specs=[VMEM, VMEM, HBM, HBM],
        out_specs=[HBM] * count,
        scratch_shapes=[
            pltpu.VMEM((count, both, width), BF16),
            pltpu.VMEM((count, both, width), BF16),
            pltpu.VMEM((count, rows, width), BF16),
            dma,
            dma,
            dma,
        ],
        compiler_params=params(12),
        cost_estimate=cost(
            rows, 2 * both, count * width, count * 2 * width * (rows + 2 * both) * 2
        ),
        name="partial",
    )(grads, other, *pin((own_w, other_w)))


def down_total_kernel(order, *refs):
    pieces = refs[:8]
    active, grad_down, rows_grad, out, row_sem, out_sem = refs[8:]
    width = out.shape[2]
    for copy in piece_copies(pieces, rows_grad, row_sem):
        copy.start()

    def step(j, carry):
        wait_for(rows_grad.at[j], row_sem.at[j])
        out[j] = jnp.dot(active[...], rows_grad[j], preferred_element_type=F32).astype(BF16)
        at = pl.ds(pl.multiple_of(order[j] * width, width), width)
        pltpu.make_async_copy(out.at[j], grad_down.at[:, at], out_sem.at[j]).start()
        return carry

    lax.fori_loop(0, 8, step, 0)
    finish(out, out_sem)


def down_total_call(order, pieces, active):
    width = pieces[0].shape[1]
    hidden, rows = active.shape
    dma = pltpu.SemaphoreType.DMA((8,))
    return pl.pallas_call(
        down_total_kernel,
        out_shape=jax.ShapeDtypeStruct((hidden, 8 * width), BF16),
        in_specs=[SMEM] + [HBM] * 8 + [VMEM],
        out_specs=HBM,
        scratch_shapes=[
            pltpu.VMEM((8, rows, width), BF16),
            pltpu.VMEM((8, hidden, width), BF16),
            dma,
            dma,
        ],
        compiler_params=params(12),
        cost_estimate=cost(rows, 8 * width, hidden, 8 * width * (rows + hidden) * 2),
        name="down_total",
    )(order, *pin(pieces), active)


def gate_up_total_kernel(order, *refs):
    pieces = refs[:8]
    grads, grad_gate, grad_up, rows_in, out_gate, out_up, row_sem, gate_sem, up_sem = refs[8:]
    width, hidden = out_gate.shape[1:]
    for copy in piece_copies(pieces, rows_in, row_sem):
        copy.start()

    def step(j, carry):
        wait_for(rows_in.at[j], row_sem.at[j])
        both = lax.dot_general(
            rows_in[j], grads[...], (((0,), (0,)), ((), ())), preferred_element_type=F32
        )
        out_gate[j] = both[:, :hidden].astype(BF16)
        out_up[j] = both[:, hidden:].astype(BF16)
        at = pl.ds(pl.multiple_of(order[j] * width, width), width)
        pltpu.make_async_copy(out_gate.at[j], grad_gate.at[at, :], gate_sem.at[j]).start()
        pltpu.make_async_copy(out_up.at[j], grad_up.at[at, :], up_sem.at[j]).start()
        return carry

    lax.fori_loop(0, 8, step, 0)
    finish(out_gate, gate_sem)
    finish(out_up, up_sem)


def gate_up_total_call(order, pieces, grads):
    width = pieces[0].shape[1]
    rows, both = grads.shape
    hidden = both // 2
    dma = pltpu.SemaphoreType.DMA((8,))
    total = jax.ShapeDtypeStruct((8 * width, hidden), BF16)
    return pl.pallas_call(
        gate_up_total_kernel,
        out_shape=(total, total),
        in_specs=[SMEM] + [HBM] * 8 + [VMEM],
        out_specs=(HBM, HBM),
        scratch_shapes=[
            pltpu.VMEM((8, rows, width), BF16),
            pltpu.VMEM((8, width, hidden), BF16),
            pltpu.VMEM((8, width, hidden), BF16),
            dma,
            dma,
            dma,
        ],
        compiler_params=params(16),
        cost_estimate=cost(rows, 8 * width, both, 8 * width * (rows + both) * 2),
        name="gate_up_total",
    )(order, *pin(pieces), grads)


def body(tokens_in, grad_out, expert_ids, w_gate, w_up, w_down):
    experts = lax.axis_size("node")
    token_count, topk = expert_ids.shape
    capacity = token_count * topk * 3 // (2 * experts)
    places = slot_places(expert_ids, experts)
    onehot = slot_onehot(places, 0, capacity)

    def packed(table):
        return jnp.dot(onehot, table, preferred_element_type=F32).astype(BF16)

    def exchange(value):
        return lax.all_to_all(value, "node", split_axis=0, concat_axis=0, tiled=True)

    packed_grad = packed(grad_out)
    order = after(ring_order(), packed_grad)
    w_gu, own_w, send_w, w_dn = prepare_call(order, w_gate[0], w_up[0], w_down[0])
    arrived_in = after(exchange(packed(tokens_in)), w_gu)
    arrived_grad = exchange(after(packed_grad, arrived_in))
    near_in, far_in = ring_gather(arrived_in)
    pieces_in = (*near_in, far_in, core_swap(far_in))
    other_w = core_swap(after(send_w, near_in[2]))
    active, swish, slope = gate_up_call(pieces_in, w_gu)
    near_grad, far_grad = ring_gather(after(arrived_grad, far_in), (active,))
    before = hidden_start_call(near_grad, w_dn)
    far_grad = after(far_grad, before)
    far_grad = (far_grad, core_swap(far_grad))
    pieces_grad = (*near_grad, *far_grad)
    grads = hidden_end_call(far_grad, w_dn, before, swish, slope)
    other = core_swap(grads)

    def partial_of(*blocks):
        return partial_call(grads, other, own_w, other_w, blocks)

    far = chip_step(partial_of(3)[0], 1)
    back = chip_step(partial_of(1)[0], -1)
    own, on = partial_of(0, 2)
    down_total = down_total_call(order, pieces_grad, active.T)
    joined = on.astype(F32) + after(far, down_total).astype(F32)
    on = chip_step(joined.astype(BF16), 1)
    total = (own.astype(F32) + back.astype(F32) + on.astype(F32)).astype(BF16)

    gate_total, up_total = gate_up_total_call(order, pieces_in, grads)
    returned = exchange(after(total, gate_total))
    grad_in = jnp.einsum("st,sd->td", onehot, returned, preferred_element_type=F32)
    return (grad_in.astype(BF16), gate_total[None], up_total[None], down_total[None])


def solution(mesh):
    placed = (
        P("node", "local"),
        P("node", "local"),
        P("node", None),
        P("node", None, "local"),
        P("node", None, "local"),
        P("node", "local", None),
    )
    return jax.shard_map(
        body,
        mesh=mesh,
        in_specs=placed,
        out_specs=(
            P("node", "local"),
            P("node", None, "local"),
            P("node", None, "local"),
            P("node", "local", None),
        ),
        check_vma=False,
    )
```

```python
import functools

import jax
import jax.numpy as jnp
from jax import lax
from jax.experimental import pallas as pl
from jax.experimental.pallas import tpu as pltpu
from jax.sharding import PartitionSpec as P

F32 = jnp.float32
BF16 = jnp.bfloat16
ANY = pl.BlockSpec(memory_space=pl.ANY)
HBM = pl.BlockSpec(memory_space=pltpu.HBM)
SMEM = pl.BlockSpec(memory_space=pltpu.SMEM)
VMEM = pl.BlockSpec(memory_space=pltpu.VMEM)
MIB = 1024 * 1024


def slot_places(block_ids, experts):
    tokens = block_ids.shape[0]
    named = jnp.sum(
        (block_ids[:, :, None] == jnp.arange(experts, dtype=jnp.int32)).astype(BF16), axis=1
    )
    row = lax.broadcasted_iota(jnp.int32, (tokens, tokens), 0)
    column = lax.broadcasted_iota(jnp.int32, (tokens, tokens), 1)
    before = (column < row).astype(BF16)
    earlier = jnp.einsum("se,ts->et", named, before, preferred_element_type=F32)
    return jnp.where(named.T > 0, earlier.astype(jnp.int32), -1)


def slot_onehot(places, first, count):
    experts, tokens = places.shape
    slot = first + jnp.arange(count, dtype=jnp.int32)
    onehot = (places[:, None, :] == slot[None, :, None]).astype(BF16)
    return onehot.reshape(experts * count, tokens)


def chip_step(value, step):
    size = lax.axis_size("local")
    chips = size // 2
    pairs = []
    for y in range(chips):
        pairs.append((2 * y, 2 * ((y + step) % chips)))
        pairs.append((2 * y + 1, 2 * ((y - step) % chips) + 1))
    return lax.ppermute(value, "local", pairs)


def core_swap(value):
    return lax.ppermute(value, "local", [(i, i ^ 1) for i in range(lax.axis_size("local"))])


def pin(values):
    return [pltpu.with_memory_space_constraint(value, pltpu.HBM) for value in values]


def after(value, *others):
    return lax.optimization_barrier((value, *others))[0]


def ring_gather(own, beside=(), between=()):
    back = chip_step(own, 1)
    on = chip_step(after(own, *beside), -1)
    far = chip_step(after(back, *between), 1)
    return back, on, far


def ring_order():
    size = lax.axis_size("local")
    chips = size // 2
    me = lax.axis_index("local")
    chip, core = me // 2, me % 2
    blocks = []
    for step in (0, -1, 1, 2):
        for other in (0, 1):
            from_core = (core + other) % 2
            moved = step * (1 - 2 * from_core)
            blocks.append(2 * ((chip + moved + chips) % chips) + from_core)
    return jnp.stack(blocks).astype(jnp.int32)


def piece_copies(pieces, buffer, sem):
    return [pltpu.make_async_copy(pieces[j], buffer.at[j], sem.at[j]) for j in range(8)]


def wait_for(ref, sem):
    pltpu.make_async_copy(ref, ref, sem).wait()


def finish(outs, sem):
    def step(j, carry):
        wait_for(outs.at[j], sem.at[j])
        return carry

    lax.fori_loop(0, outs.shape[0], step, 0)


def cost(rows, depth, columns, moved):
    return pl.CostEstimate(
        flops=2 * rows * depth * columns, bytes_accessed=moved, transcendentals=0
    )


def params(mib):
    return pltpu.CompilerParams(vmem_limit_bytes=mib * MIB)


def prepare_kernel(order, gate_a, gate_b, up_a, up_b, down_a, down_b, w_gu, own_t, send_t, w_dn):
    del order
    hidden = gate_a.shape[1]
    for i, (gate, up, down, turned) in enumerate(
        ((gate_a, up_a, down_a, own_t), (gate_b, up_b, down_b, send_t))
    ):
        w_gu[i, :, :hidden] = gate[...]
        w_gu[i, :, hidden:] = up[...]
        turned[0, :hidden, :] = gate[...].T
        turned[0, hidden:, :] = up[...].T
        w_dn[i] = down[...].T


def prepare_call(order, w_gate, w_up, w_down):
    depth, hidden = w_gate.shape
    width = depth // 8

    def rows(core):
        return pl.BlockSpec((width, hidden), lambda d, order: (order[2 * d + core], 0))

    def columns(core):
        return pl.BlockSpec((hidden, width), lambda d, order: (0, order[2 * d + core]))

    def out(count, *shape):
        return pl.BlockSpec((count, *shape), lambda d, order: (d, 0, 0))

    turned = pltpu.HBM((4, 2 * hidden, width), BF16)
    return pl.pallas_call(
        prepare_kernel,
        out_shape=(
            pltpu.HBM((8, width, 2 * hidden), BF16),
            turned,
            turned,
            pltpu.HBM((8, width, hidden), BF16),
        ),
        grid_spec=pltpu.PrefetchScalarGridSpec(
            num_scalar_prefetch=1,
            grid=(4,),
            in_specs=[rows(0), rows(1), rows(0), rows(1), columns(0), columns(1)],
            out_specs=(
                out(2, width, 2 * hidden),
                out(1, 2 * hidden, width),
                out(1, 2 * hidden, width),
                out(2, width, hidden),
            ),
        ),
        compiler_params=params(14),
        cost_estimate=cost(depth, hidden, 768, depth * hidden * 16),
        name="prepare",
    )(order, *pin((w_gate, w_gate, w_up, w_up, w_down, w_down)))


def gate_up_kernel(*refs):
    pieces, weights = refs[:8], refs[8]
    active, factors, rows_in, w_gu, acc, row_sem, w_sem = refs[9:]
    hidden = active.shape[1]
    for j in range(8):
        pltpu.make_async_copy(weights.at[j], w_gu.at[j], w_sem.at[j]).start()
    for copy in piece_copies(pieces, rows_in, row_sem):
        copy.start()
    acc[...] = jnp.zeros_like(acc)

    def step(j, carry):
        wait_for(w_gu.at[j], w_sem.at[j])
        wait_for(rows_in.at[j], row_sem.at[j])
        acc[...] += jnp.dot(rows_in[j], w_gu[j], preferred_element_type=F32)
        return carry

    lax.fori_loop(0, 8, step, 0)
    gate_pre = acc[:, :hidden]
    up_pre = acc[:, hidden:]
    sigmoid_gate = jax.nn.sigmoid(gate_pre)
    swish_gate = gate_pre * sigmoid_gate
    active[...] = (swish_gate * up_pre).astype(BF16)
    factors[:, :hidden] = up_pre * sigmoid_gate * (1.0 + gate_pre * (1.0 - sigmoid_gate))
    factors[:, hidden:] = swish_gate


def gate_up_call(pieces, w_gu):
    rows, width = pieces[0].shape
    both = w_gu.shape[2]
    hidden = both // 2
    dma = pltpu.SemaphoreType.DMA((8,))
    return pl.pallas_call(
        gate_up_kernel,
        out_shape=(
            jax.ShapeDtypeStruct((rows, hidden), BF16),
            jax.ShapeDtypeStruct((rows, both), F32),
        ),
        in_specs=[HBM] * 9,
        out_specs=(VMEM, VMEM),
        scratch_shapes=[
            pltpu.VMEM((8, rows, width), BF16),
            pltpu.VMEM((8, width, both), BF16),
            pltpu.VMEM((rows, both), F32),
            dma,
            dma,
        ],
        compiler_params=params(16),
        cost_estimate=cost(rows, 8 * width, both, 8 * width * (rows + both) * 2),
        name="gate_up",
    )(*pin((*pieces, w_gu)))


def add_hidden(first, pieces, own_w, other_w, total, rows_grad, w_dn, row_sem, own_sem, other_sem):
    count = len(pieces)
    hidden = own_w.shape[2]
    for j in range(count):
        own = w_dn.at[j, :, pl.ds(0, hidden)]
        other = w_dn.at[j, :, pl.ds(hidden, hidden)]
        pltpu.make_async_copy(own_w.at[first + j], own, own_sem.at[j]).start()
        pltpu.make_async_copy(other_w.at[(first + j) ^ 1], other, other_sem.at[j]).start()
        pltpu.make_async_copy(pieces[j], rows_grad.at[j], row_sem.at[j]).start()

    def step(j, carry):
        wait_for(own_w.at[0], own_sem.at[j])
        wait_for(other_w.at[0], other_sem.at[j])
        wait_for(rows_grad.at[j], row_sem.at[j])
        total[...] += jnp.dot(rows_grad[j], w_dn[j], preferred_element_type=F32)
        return carry

    lax.fori_loop(0, count, step, 0)


def hidden_start_kernel(count, *refs):
    total = refs[count + 2]
    total[...] = jnp.zeros_like(total)
    add_hidden(0, refs[:count], *refs[count : count + 3], *refs[count + 3 :])


def hidden_start_call(pieces, own_w, other_w):
    rows, width = pieces[0].shape
    both, count = 2 * own_w.shape[2], len(pieces)
    dma = pltpu.SemaphoreType.DMA((count,))
    return pl.pallas_call(
        functools.partial(hidden_start_kernel, count),
        out_shape=jax.ShapeDtypeStruct((rows, both), F32),
        in_specs=[ANY] * count + [HBM] * 2,
        out_specs=VMEM,
        scratch_shapes=[
            pltpu.VMEM((count, rows, width), BF16),
            pltpu.VMEM((count, width, both), BF16),
            dma,
            dma,
            dma,
        ],
        compiler_params=params(16),
        cost_estimate=cost(rows, count * width, both, count * width * (rows + both) * 2),
        name="hidden_start",
    )(*pieces, *pin((own_w, other_w)))


def start_weights(own_w, other_w, block, buffer, own_sem, other_sem):
    both = own_w.shape[1]
    pltpu.make_async_copy(own_w.at[block], buffer.at[pl.ds(0, both), :], own_sem).start()
    pltpu.make_async_copy(other_w.at[block], buffer.at[pl.ds(both, both), :], other_sem).start()


def hidden_end_kernel(first, count, block, *refs):
    pieces = refs[:count]
    own_dn, other_dn, own_w, other_w, before, own_factors, other_factors = refs[count : count + 7]
    grads, out = refs[count + 7 : count + 9]
    total, rows_grad, w_dn, w_gu, result = refs[count + 9 : count + 14]
    row_sem, own_sem, other_sem, w_sem, out_sem = refs[count + 14 :]
    start_weights(own_w, other_w, block, w_gu, w_sem.at[0], w_sem.at[1])
    total[...] = before[...]
    add_hidden(
        first, pieces, own_dn, other_dn, total, rows_grad, w_dn, row_sem, own_sem, other_sem
    )
    hidden = own_dn.shape[2]
    for core, factors in enumerate((own_factors, other_factors)):
        hidden_grad = total[:, core * hidden : (core + 1) * hidden]
        at = 2 * core * hidden
        grads[:, at : at + hidden] = (hidden_grad * factors[:, :hidden]).astype(BF16)
        grads[:, at + hidden : at + 2 * hidden] = (hidden_grad * factors[:, hidden:]).astype(BF16)
    wait_for(own_w.at[0], w_sem.at[0])
    wait_for(other_w.at[0], w_sem.at[1])
    result[...] = jnp.dot(grads[...], w_gu[...], preferred_element_type=F32).astype(BF16)
    copy = pltpu.make_async_copy(result, out, out_sem)
    copy.start()
    copy.wait()


def hidden_end_call(pieces, own_dn, other_dn, own_w, other_w, before, factors, others, block):
    rows, width = pieces[0].shape
    both, count = 2 * own_dn.shape[2], len(pieces)
    dma = pltpu.SemaphoreType.DMA
    return pl.pallas_call(
        functools.partial(hidden_end_kernel, own_dn.shape[0] - count, count, block),
        out_shape=(
            jax.ShapeDtypeStruct((rows, 2 * both), BF16),
            pltpu.HBM((rows, width), BF16),
        ),
        in_specs=[ANY] * count + [HBM] * 4 + [VMEM] * 3,
        out_specs=(VMEM, HBM),
        scratch_shapes=[
            pltpu.VMEM((rows, both), F32),
            pltpu.VMEM((count, rows, width), BF16),
            pltpu.VMEM((count, width, both), BF16),
            pltpu.VMEM((2 * both, width), BF16),
            pltpu.VMEM((rows, width), BF16),
            dma((count,)),
            dma((count,)),
            dma((count,)),
            dma((2,)),
            dma,
        ],
        compiler_params=params(20),
        cost_estimate=cost(rows, (count + 2) * width, both, count * width * (rows + both) * 2),
        name="hidden_end",
    )(*pieces, *pin((own_dn, other_dn, own_w, other_w)), before, factors, others)


def partial_kernel(blocks, *refs):
    count = len(blocks)
    grads, own_w, other_w = refs[:3]
    outs = refs[3 : 3 + count]
    w_gu, result, own_sem, other_sem, out_sem = refs[3 + count :]
    for i, j in enumerate(blocks):
        start_weights(own_w, other_w, j, w_gu.at[i], own_sem.at[i], other_sem.at[i])
    for i in range(count):
        wait_for(own_w.at[0], own_sem.at[i])
        wait_for(other_w.at[0], other_sem.at[i])
        result[i] = jnp.dot(grads[...], w_gu[i], preferred_element_type=F32).astype(BF16)
        pltpu.make_async_copy(result.at[i], outs[i], out_sem.at[i]).start()
    finish(result, out_sem)


def partial_call(grads, own_w, other_w, blocks):
    both, width = own_w.shape[1:]
    rows, count = grads.shape[0], len(blocks)
    dma = pltpu.SemaphoreType.DMA((count,))
    return pl.pallas_call(
        functools.partial(partial_kernel, blocks),
        out_shape=[pltpu.HBM((rows, width), BF16)] * count,
        in_specs=[VMEM, HBM, HBM],
        out_specs=[HBM] * count,
        scratch_shapes=[
            pltpu.VMEM((count, 2 * both, width), BF16),
            pltpu.VMEM((count, rows, width), BF16),
            dma,
            dma,
            dma,
        ],
        compiler_params=params(14),
        cost_estimate=cost(
            rows, 2 * both, count * width, count * 2 * width * (rows + 2 * both) * 2
        ),
        name="partial",
    )(grads, *pin((own_w, other_w)))


def down_total_kernel(order, *refs):
    pieces = refs[:8]
    active, grad_down, rows_grad, out, row_sem, out_sem = refs[8:]
    width = out.shape[2]
    for copy in piece_copies(pieces, rows_grad, row_sem):
        copy.start()

    def step(j, carry):
        wait_for(rows_grad.at[j], row_sem.at[j])
        out[j] = jnp.dot(active[...], rows_grad[j], preferred_element_type=F32).astype(BF16)
        at = pl.ds(pl.multiple_of(order[j] * width, width), width)
        pltpu.make_async_copy(out.at[j], grad_down.at[:, at], out_sem.at[j]).start()
        return carry

    lax.fori_loop(0, 8, step, 0)
    finish(out, out_sem)


def down_total_call(order, pieces, active):
    width = pieces[0].shape[1]
    hidden, rows = active.shape
    dma = pltpu.SemaphoreType.DMA((8,))
    return pl.pallas_call(
        down_total_kernel,
        out_shape=jax.ShapeDtypeStruct((hidden, 8 * width), BF16),
        in_specs=[SMEM] + [HBM] * 8 + [VMEM],
        out_specs=HBM,
        scratch_shapes=[
            pltpu.VMEM((8, rows, width), BF16),
            pltpu.VMEM((8, hidden, width), BF16),
            dma,
            dma,
        ],
        compiler_params=params(12),
        cost_estimate=cost(rows, 8 * width, hidden, 8 * width * (rows + hidden) * 2),
        name="down_total",
    )(order, *pin(pieces), active)


def gate_up_total_kernel(order, *refs):
    pieces = refs[:8]
    grads, grad_gate, grad_up, rows_in, out_gate, out_up, row_sem, gate_sem, up_sem = refs[8:]
    width, hidden = out_gate.shape[1:]
    for copy in piece_copies(pieces, rows_in, row_sem):
        copy.start()

    def step(j, carry):
        wait_for(rows_in.at[j], row_sem.at[j])
        both = lax.dot_general(
            rows_in[j],
            grads[:, : 2 * hidden],
            (((0,), (0,)), ((), ())),
            preferred_element_type=F32,
        )
        out_gate[j] = both[:, :hidden].astype(BF16)
        out_up[j] = both[:, hidden:].astype(BF16)
        at = pl.ds(pl.multiple_of(order[j] * width, width), width)
        pltpu.make_async_copy(out_gate.at[j], grad_gate.at[at, :], gate_sem.at[j]).start()
        pltpu.make_async_copy(out_up.at[j], grad_up.at[at, :], up_sem.at[j]).start()
        return carry

    lax.fori_loop(0, 8, step, 0)
    finish(out_gate, gate_sem)
    finish(out_up, up_sem)


def gate_up_total_call(order, pieces, grads):
    width = pieces[0].shape[1]
    rows, both = grads.shape[0], grads.shape[1] // 2
    hidden = both // 2
    dma = pltpu.SemaphoreType.DMA((8,))
    total = jax.ShapeDtypeStruct((8 * width, hidden), BF16)
    return pl.pallas_call(
        gate_up_total_kernel,
        out_shape=(total, total),
        in_specs=[SMEM] + [HBM] * 8 + [VMEM],
        out_specs=(HBM, HBM),
        scratch_shapes=[
            pltpu.VMEM((8, rows, width), BF16),
            pltpu.VMEM((8, width, hidden), BF16),
            pltpu.VMEM((8, width, hidden), BF16),
            dma,
            dma,
            dma,
        ],
        compiler_params=params(16),
        cost_estimate=cost(rows, 8 * width, both, 8 * width * (rows + both) * 2),
        name="gate_up_total",
    )(order, *pin(pieces), grads)


def body(tokens_in, grad_out, expert_ids, w_gate, w_up, w_down):
    experts = lax.axis_size("node")
    token_count, topk = expert_ids.shape
    capacity = token_count * topk * 3 // (2 * experts)
    places = slot_places(expert_ids, experts)
    onehot = slot_onehot(places, 0, capacity)

    def packed(table):
        return jnp.dot(onehot, table, preferred_element_type=F32).astype(BF16)

    def exchange(value):
        return lax.all_to_all(value, "node", split_axis=0, concat_axis=0, tiled=True)

    packed_grad = packed(grad_out)
    order = after(ring_order(), packed_grad)
    w_gu, own_w, send_w, w_dn = prepare_call(order, w_gate[0], w_up[0], w_down[0])
    arrived_in = after(exchange(packed(tokens_in)), w_gu)
    arrived_grad = exchange(after(packed_grad, arrived_in))
    back, on, far = ring_gather(arrived_in)
    pieces_in = (arrived_in, core_swap(arrived_in), back, core_swap(back), on, core_swap(on))
    pieces_in = (*pieces_in, far, core_swap(far))
    other_w = core_swap(after(send_w, back))
    other_dn = core_swap(after(w_dn, back))
    active, factors = gate_up_call(pieces_in, w_gu)
    back, on, far = ring_gather(after(arrived_grad, far))
    others = core_swap(factors)
    near = (arrived_grad, core_swap(arrived_grad), back, core_swap(back), on, core_swap(on))
    before = hidden_start_call(near, w_dn, other_dn)
    far = after(far, before, active)
    late = (far, core_swap(far))
    pieces_grad = (*near, *late)
    grads, far = hidden_end_call(
        late, w_dn, other_dn, own_w, other_w, before, factors, others, 3
    )
    far = chip_step(far, 1)
    back, own, on = partial_call(grads, own_w, other_w, (1, 0, 2))
    back = chip_step(back, -1)
    joined = on.astype(F32) + far.astype(F32)
    on = chip_step(joined.astype(BF16), 1)
    total = (own.astype(F32) + back.astype(F32) + on.astype(F32)).astype(BF16)
    down_total = down_total_call(order, pieces_grad, active.T)
    gate_total, up_total = gate_up_total_call(order, pieces_in, grads)
    returned = exchange(total)
    grad_in = jnp.einsum("st,sd->td", onehot, returned, preferred_element_type=F32)
    return (grad_in.astype(BF16), gate_total[None], up_total[None], down_total[None])


def solution(mesh):
    placed = (
        P("node", "local"),
        P("node", "local"),
        P("node", None),
        P("node", None, "local"),
        P("node", None, "local"),
        P("node", "local", None),
    )
    return jax.shard_map(
        body,
        mesh=mesh,
        in_specs=placed,
        out_specs=(
            P("node", "local"),
            P("node", None, "local"),
            P("node", None, "local"),
            P("node", "local", None),
        ),
        check_vma=False,
    )
```

```python
import functools

import jax
import jax.numpy as jnp
from jax import lax
from jax.experimental import pallas as pl
from jax.experimental.pallas import tpu as pltpu
from jax.sharding import PartitionSpec as P

F32 = jnp.float32
BF16 = jnp.bfloat16
ANY = pl.BlockSpec(memory_space=pl.ANY)
HBM = pl.BlockSpec(memory_space=pltpu.HBM)
SMEM = pl.BlockSpec(memory_space=pltpu.SMEM)
VMEM = pl.BlockSpec(memory_space=pltpu.VMEM)
MIB = 1024 * 1024


def slot_places(block_ids, experts):
    tokens = block_ids.shape[0]
    named = jnp.sum(
        (block_ids[:, :, None] == jnp.arange(experts, dtype=jnp.int32)).astype(BF16), axis=1
    )
    row = lax.broadcasted_iota(jnp.int32, (tokens, tokens), 0)
    column = lax.broadcasted_iota(jnp.int32, (tokens, tokens), 1)
    before = (column < row).astype(BF16)
    earlier = jnp.einsum("se,ts->et", named, before, preferred_element_type=F32)
    return jnp.where(named.T > 0, earlier.astype(jnp.int32), -1)


def slot_onehot(places, first, count):
    experts, tokens = places.shape
    slot = first + jnp.arange(count, dtype=jnp.int32)
    onehot = (places[:, None, :] == slot[None, :, None]).astype(BF16)
    return onehot.reshape(experts * count, tokens)


def chip_step(value, step):
    size = lax.axis_size("local")
    chips = size // 2
    pairs = []
    for y in range(chips):
        pairs.append((2 * y, 2 * ((y + step) % chips)))
        pairs.append((2 * y + 1, 2 * ((y - step) % chips) + 1))
    return lax.ppermute(value, "local", pairs)


def core_swap(value):
    return lax.ppermute(value, "local", [(i, i ^ 1) for i in range(lax.axis_size("local"))])


def pin(values):
    return [pltpu.with_memory_space_constraint(value, pltpu.HBM) for value in values]


def after(value, *others):
    return lax.optimization_barrier((value, *others))[0]


def ring_gather(own, beside=(), between=()):
    back = chip_step(own, 1)
    on = chip_step(after(own, *beside), -1)
    far = chip_step(after(back, *between), 1)
    return back, on, far


def ring_order():
    size = lax.axis_size("local")
    chips = size // 2
    me = lax.axis_index("local")
    chip, core = me // 2, me % 2
    blocks = []
    for step in (0, -1, 1, 2):
        for other in (0, 1):
            from_core = (core + other) % 2
            moved = step * (1 - 2 * from_core)
            blocks.append(2 * ((chip + moved + chips) % chips) + from_core)
    return jnp.stack(blocks).astype(jnp.int32)


def piece_copies(pieces, buffer, sem):
    return [pltpu.make_async_copy(pieces[j], buffer.at[j], sem.at[j]) for j in range(8)]


def wait_for(ref, sem):
    pltpu.make_async_copy(ref, ref, sem).wait()


def finish(outs, sem):
    def step(j, carry):
        wait_for(outs.at[j], sem.at[j])
        return carry

    lax.fori_loop(0, outs.shape[0], step, 0)


def cost(rows, depth, columns, moved):
    return pl.CostEstimate(
        flops=2 * rows * depth * columns, bytes_accessed=moved, transcendentals=0
    )


def params(mib):
    return pltpu.CompilerParams(vmem_limit_bytes=mib * MIB)


def prepare_kernel(order, gate_a, gate_b, up_a, up_b, down_a, down_b, w_gu, own_t, send_t, w_dn):
    del order
    hidden = gate_a.shape[1]
    for i, (gate, up, down, turned) in enumerate(
        ((gate_a, up_a, down_a, own_t), (gate_b, up_b, down_b, send_t))
    ):
        w_gu[i, :, :hidden] = gate[...]
        w_gu[i, :, hidden:] = up[...]
        turned[0, :hidden, :] = gate[...].T
        turned[0, hidden:, :] = up[...].T
        w_dn[i] = down[...].T


def prepare_call(order, w_gate, w_up, w_down):
    depth, hidden = w_gate.shape
    width = depth // 8

    def rows(core):
        return pl.BlockSpec((width, hidden), lambda d, order: (order[2 * d + core], 0))

    def columns(core):
        return pl.BlockSpec((hidden, width), lambda d, order: (0, order[2 * d + core]))

    def out(count, *shape):
        return pl.BlockSpec((count, *shape), lambda d, order: (d, 0, 0))

    turned = pltpu.HBM((4, 2 * hidden, width), BF16)
    return pl.pallas_call(
        prepare_kernel,
        out_shape=(
            pltpu.HBM((8, width, 2 * hidden), BF16),
            turned,
            turned,
            pltpu.HBM((8, width, hidden), BF16),
        ),
        grid_spec=pltpu.PrefetchScalarGridSpec(
            num_scalar_prefetch=1,
            grid=(4,),
            in_specs=[rows(0), rows(1), rows(0), rows(1), columns(0), columns(1)],
            out_specs=(
                out(2, width, 2 * hidden),
                out(1, 2 * hidden, width),
                out(1, 2 * hidden, width),
                out(2, width, hidden),
            ),
        ),
        compiler_params=params(14),
        cost_estimate=cost(depth, hidden, 768, depth * hidden * 16),
        name="prepare",
    )(order, *pin((w_gate, w_gate, w_up, w_up, w_down, w_down)))


def gate_up_kernel(*refs):
    pieces, weights = refs[:8], refs[8]
    active, factors, rows_in, w_gu, acc, row_sem, w_sem = refs[9:]
    hidden = active.shape[1]
    for j in range(8):
        pltpu.make_async_copy(weights.at[j], w_gu.at[j], w_sem.at[j]).start()
    for copy in piece_copies(pieces, rows_in, row_sem):
        copy.start()
    acc[...] = jnp.zeros_like(acc)

    def step(j, carry):
        wait_for(w_gu.at[j], w_sem.at[j])
        wait_for(rows_in.at[j], row_sem.at[j])
        acc[...] += jnp.dot(rows_in[j], w_gu[j], preferred_element_type=F32)
        return carry

    lax.fori_loop(0, 8, step, 0)
    gate_pre = acc[:, :hidden]
    up_pre = acc[:, hidden:]
    sigmoid_gate = jax.nn.sigmoid(gate_pre)
    swish_gate = gate_pre * sigmoid_gate
    active[...] = (swish_gate * up_pre).astype(BF16)
    factors[:, :hidden] = up_pre * sigmoid_gate * (1.0 + gate_pre * (1.0 - sigmoid_gate))
    factors[:, hidden:] = swish_gate


def gate_up_call(pieces, w_gu):
    rows, width = pieces[0].shape
    both = w_gu.shape[2]
    hidden = both // 2
    dma = pltpu.SemaphoreType.DMA((8,))
    return pl.pallas_call(
        gate_up_kernel,
        out_shape=(
            jax.ShapeDtypeStruct((rows, hidden), BF16),
            jax.ShapeDtypeStruct((rows, both), F32),
        ),
        in_specs=[HBM] * 9,
        out_specs=(VMEM, VMEM),
        scratch_shapes=[
            pltpu.VMEM((8, rows, width), BF16),
            pltpu.VMEM((8, width, both), BF16),
            pltpu.VMEM((rows, both), F32),
            dma,
            dma,
        ],
        compiler_params=params(16),
        cost_estimate=cost(rows, 8 * width, both, 8 * width * (rows + both) * 2),
        name="gate_up",
    )(*pin((*pieces, w_gu)))


def add_hidden(first, pieces, own_w, other_w, total, w_dn, own_sem, other_sem):
    count = len(pieces)
    hidden = own_w.shape[2]
    for j in range(count):
        own = w_dn.at[j, :, pl.ds(0, hidden)]
        other = w_dn.at[j, :, pl.ds(hidden, hidden)]
        pltpu.make_async_copy(own_w.at[first + j], own, own_sem.at[j]).start()
        pltpu.make_async_copy(other_w.at[(first + j) ^ 1], other, other_sem.at[j]).start()
    for j in range(count):
        wait_for(own_w.at[0], own_sem.at[j])
        wait_for(other_w.at[0], other_sem.at[j])
        total[...] += jnp.dot(pieces[j][...], w_dn[j], preferred_element_type=F32)


def hidden_start_kernel(count, *refs):
    pieces, weights, total, rows_grad, w_dn, row_sem, w_sem = refs[:count], *refs[count:]
    for j in range(count):
        pltpu.make_async_copy(weights.at[j], w_dn.at[j], w_sem.at[j]).start()
        pltpu.make_async_copy(pieces[j], rows_grad.at[j], row_sem.at[j]).start()
    total[...] = jnp.zeros_like(total)

    def step(j, carry):
        wait_for(w_dn.at[j], w_sem.at[j])
        wait_for(rows_grad.at[j], row_sem.at[j])
        total[...] += jnp.dot(rows_grad[j], w_dn[j], preferred_element_type=F32)
        return carry

    lax.fori_loop(0, count, step, 0)


def hidden_start_call(pieces, w_dn):
    rows, width = pieces[0].shape
    hidden, count = w_dn.shape[2], len(pieces)
    dma = pltpu.SemaphoreType.DMA((count,))
    return pl.pallas_call(
        functools.partial(hidden_start_kernel, count),
        out_shape=jax.ShapeDtypeStruct((rows, hidden), F32),
        in_specs=[ANY] * count + [HBM],
        out_specs=VMEM,
        scratch_shapes=[
            pltpu.VMEM((count, rows, width), BF16),
            pltpu.VMEM((count, width, hidden), BF16),
            dma,
            dma,
        ],
        compiler_params=params(15),
        cost_estimate=cost(rows, count * width, hidden, count * width * (rows + hidden) * 2),
        name="hidden_start",
    )(*pieces, *pin((w_dn,)))


def start_weights(own_w, other_w, block, buffer, own_sem, other_sem):
    both = own_w.shape[1]
    pltpu.make_async_copy(own_w.at[block], buffer.at[pl.ds(0, both), :], own_sem).start()
    pltpu.make_async_copy(other_w.at[block], buffer.at[pl.ds(both, both), :], other_sem).start()


def hidden_end_kernel(first, count, block, *refs):
    pieces = refs[:count]
    own_dn, other_dn, own_w, other_w = refs[count : count + 4]
    before, other_before, own_factors, other_factors = refs[count + 4 : count + 8]
    grads, out = refs[count + 8 : count + 10]
    total, w_dn, w_gu, result, own_sem, other_sem, w_sem, out_sem = refs[count + 10 :]
    start_weights(own_w, other_w, block, w_gu, w_sem.at[0], w_sem.at[1])
    half = before.shape[1]
    total[:, :half] = before[...]
    total[:, half:] = other_before[...]
    add_hidden(first, pieces, own_dn, other_dn, total, w_dn, own_sem, other_sem)
    hidden = own_dn.shape[2]
    for core, factors in enumerate((own_factors, other_factors)):
        hidden_grad = total[:, core * hidden : (core + 1) * hidden]
        at = 2 * core * hidden
        grads[:, at : at + hidden] = (hidden_grad * factors[:, :hidden]).astype(BF16)
        grads[:, at + hidden : at + 2 * hidden] = (hidden_grad * factors[:, hidden:]).astype(BF16)
    wait_for(own_w.at[0], w_sem.at[0])
    wait_for(other_w.at[0], w_sem.at[1])
    result[...] = jnp.dot(grads[...], w_gu[...], preferred_element_type=F32).astype(BF16)
    copy = pltpu.make_async_copy(result, out, out_sem)
    copy.start()
    copy.wait()


def hidden_end_call(pieces, own_dn, other_dn, own_w, other_w, befores, factors, others, block):
    rows, width = pieces[0].shape
    both, count = 2 * own_dn.shape[2], len(pieces)
    dma = pltpu.SemaphoreType.DMA
    return pl.pallas_call(
        functools.partial(hidden_end_kernel, own_dn.shape[0] - count, count, block),
        out_shape=(
            jax.ShapeDtypeStruct((rows, 2 * both), BF16),
            pltpu.HBM((rows, width), BF16),
        ),
        in_specs=[VMEM] * count + [HBM] * 4 + [VMEM] * 4,
        out_specs=(VMEM, HBM),
        scratch_shapes=[
            pltpu.VMEM((rows, both), F32),
            pltpu.VMEM((count, width, both), BF16),
            pltpu.VMEM((2 * both, width), BF16),
            pltpu.VMEM((rows, width), BF16),
            dma((count,)),
            dma((count,)),
            dma((2,)),
            dma,
        ],
        compiler_params=params(20),
        cost_estimate=cost(rows, (count + 2) * width, both, count * width * (rows + both) * 2),
        name="hidden_end",
    )(*pieces, *pin((own_dn, other_dn, own_w, other_w)), *befores, factors, others)


def partial_kernel(blocks, *refs):
    count = len(blocks)
    grads, own_w, other_w = refs[:3]
    outs = refs[3 : 3 + count]
    w_gu, result, own_sem, other_sem, out_sem = refs[3 + count :]
    for i, j in enumerate(blocks):
        start_weights(own_w, other_w, j, w_gu.at[i], own_sem.at[i], other_sem.at[i])
    for i in range(count):
        wait_for(own_w.at[0], own_sem.at[i])
        wait_for(other_w.at[0], other_sem.at[i])
        result[i] = jnp.dot(grads[...], w_gu[i], preferred_element_type=F32).astype(BF16)
        pltpu.make_async_copy(result.at[i], outs[i], out_sem.at[i]).start()
    finish(result, out_sem)


def partial_call(grads, own_w, other_w, blocks):
    both, width = own_w.shape[1:]
    rows, count = grads.shape[0], len(blocks)
    dma = pltpu.SemaphoreType.DMA((count,))
    return pl.pallas_call(
        functools.partial(partial_kernel, blocks),
        out_shape=[pltpu.HBM((rows, width), BF16)] * count,
        in_specs=[VMEM, HBM, HBM],
        out_specs=[HBM] * count,
        scratch_shapes=[
            pltpu.VMEM((count, 2 * both, width), BF16),
            pltpu.VMEM((count, rows, width), BF16),
            dma,
            dma,
            dma,
        ],
        compiler_params=params(14),
        cost_estimate=cost(
            rows, 2 * both, count * width, count * 2 * width * (rows + 2 * both) * 2
        ),
        name="partial",
    )(grads, *pin((own_w, other_w)))


def down_total_kernel(order, *refs):
    pieces = refs[:8]
    active, grad_down, rows_grad, out, row_sem, out_sem = refs[8:]
    width = out.shape[2]
    for copy in piece_copies(pieces, rows_grad, row_sem):
        copy.start()

    def step(j, carry):
        wait_for(rows_grad.at[j], row_sem.at[j])
        out[j] = jnp.dot(active[...], rows_grad[j], preferred_element_type=F32).astype(BF16)
        at = pl.ds(pl.multiple_of(order[j] * width, width), width)
        pltpu.make_async_copy(out.at[j], grad_down.at[:, at], out_sem.at[j]).start()
        return carry

    lax.fori_loop(0, 8, step, 0)
    finish(out, out_sem)


def down_total_call(order, pieces, active):
    width = pieces[0].shape[1]
    hidden, rows = active.shape
    dma = pltpu.SemaphoreType.DMA((8,))
    return pl.pallas_call(
        down_total_kernel,
        out_shape=jax.ShapeDtypeStruct((hidden, 8 * width), BF16),
        in_specs=[SMEM] + [HBM] * 8 + [VMEM],
        out_specs=HBM,
        scratch_shapes=[
            pltpu.VMEM((8, rows, width), BF16),
            pltpu.VMEM((8, hidden, width), BF16),
            dma,
            dma,
        ],
        compiler_params=params(12),
        cost_estimate=cost(rows, 8 * width, hidden, 8 * width * (rows + hidden) * 2),
        name="down_total",
    )(order, *pin(pieces), active)


def gate_up_total_kernel(order, *refs):
    pieces = refs[:8]
    grads, grad_gate, grad_up, rows_in, out_gate, out_up, row_sem, gate_sem, up_sem = refs[8:]
    width, hidden = out_gate.shape[1:]
    for copy in piece_copies(pieces, rows_in, row_sem):
        copy.start()

    def step(j, carry):
        wait_for(rows_in.at[j], row_sem.at[j])
        both = lax.dot_general(
            rows_in[j],
            grads[:, : 2 * hidden],
            (((0,), (0,)), ((), ())),
            preferred_element_type=F32,
        )
        out_gate[j] = both[:, :hidden].astype(BF16)
        out_up[j] = both[:, hidden:].astype(BF16)
        at = pl.ds(pl.multiple_of(order[j] * width, width), width)
        pltpu.make_async_copy(out_gate.at[j], grad_gate.at[at, :], gate_sem.at[j]).start()
        pltpu.make_async_copy(out_up.at[j], grad_up.at[at, :], up_sem.at[j]).start()
        return carry

    lax.fori_loop(0, 8, step, 0)
    finish(out_gate, gate_sem)
    finish(out_up, up_sem)


def gate_up_total_call(order, pieces, grads):
    width = pieces[0].shape[1]
    rows, both = grads.shape[0], grads.shape[1] // 2
    hidden = both // 2
    dma = pltpu.SemaphoreType.DMA((8,))
    total = jax.ShapeDtypeStruct((8 * width, hidden), BF16)
    return pl.pallas_call(
        gate_up_total_kernel,
        out_shape=(total, total),
        in_specs=[SMEM] + [HBM] * 8 + [VMEM],
        out_specs=(HBM, HBM),
        scratch_shapes=[
            pltpu.VMEM((8, rows, width), BF16),
            pltpu.VMEM((8, width, hidden), BF16),
            pltpu.VMEM((8, width, hidden), BF16),
            dma,
            dma,
            dma,
        ],
        compiler_params=params(16),
        cost_estimate=cost(rows, 8 * width, both, 8 * width * (rows + both) * 2),
        name="gate_up_total",
    )(order, *pin(pieces), grads)


def body(tokens_in, grad_out, expert_ids, w_gate, w_up, w_down):
    experts = lax.axis_size("node")
    token_count, topk = expert_ids.shape
    capacity = token_count * topk * 3 // (2 * experts)
    places = slot_places(expert_ids, experts)
    onehot = slot_onehot(places, 0, capacity)

    def packed(table):
        return jnp.dot(onehot, table, preferred_element_type=F32).astype(BF16)

    def exchange(value):
        return lax.all_to_all(value, "node", split_axis=0, concat_axis=0, tiled=True)

    packed_grad = packed(grad_out)
    order = after(ring_order(), packed_grad)
    w_gu, own_w, send_w, w_dn = prepare_call(order, w_gate[0], w_up[0], w_down[0])
    arrived_in = after(exchange(packed(tokens_in)), w_gu)
    arrived_grad = exchange(after(packed_grad, arrived_in))
    back, on, far = ring_gather(arrived_in)
    pieces_in = (arrived_in, core_swap(arrived_in), back, core_swap(back), on, core_swap(on))
    pieces_in = (*pieces_in, far, core_swap(far))
    other_w = core_swap(after(send_w, back))
    other_dn = core_swap(after(w_dn, back))
    active, factors = gate_up_call(pieces_in, w_gu)
    back, on, far = ring_gather(after(arrived_grad, far))
    others = core_swap(factors)
    near = (arrived_grad, core_swap(arrived_grad), back, core_swap(back), on, core_swap(on))
    before = hidden_start_call(near, w_dn)
    befores = (before, core_swap(before))
    far = after(far, before, active)
    late = (far, core_swap(far))
    pieces_grad = (*near, *late)
    grads, far = hidden_end_call(
        late, w_dn, other_dn, own_w, other_w, befores, factors, others, 3
    )
    far = chip_step(far, 1)
    back, own, on = partial_call(grads, own_w, other_w, (1, 0, 2))
    back = chip_step(back, -1)
    joined = on.astype(F32) + far.astype(F32)
    on = chip_step(joined.astype(BF16), 1)
    total = (own.astype(F32) + back.astype(F32) + on.astype(F32)).astype(BF16)
    down_total = down_total_call(order, pieces_grad, active.T)
    gate_total, up_total = gate_up_total_call(order, pieces_in, grads)
    returned = exchange(total)
    grad_in = jnp.einsum("st,sd->td", onehot, returned, preferred_element_type=F32)
    return (grad_in.astype(BF16), gate_total[None], up_total[None], down_total[None])


def solution(mesh):
    placed = (
        P("node", "local"),
        P("node", "local"),
        P("node", None),
        P("node", None, "local"),
        P("node", None, "local"),
        P("node", "local", None),
    )
    return jax.shard_map(
        body,
        mesh=mesh,
        in_specs=placed,
        out_specs=(
            P("node", "local"),
            P("node", None, "local"),
            P("node", None, "local"),
            P("node", "local", None),
        ),
        check_vma=False,
    )
```

```python
import functools

import jax
import jax.numpy as jnp
from jax import lax
from jax.experimental import pallas as pl
from jax.experimental.pallas import tpu as pltpu
from jax.sharding import PartitionSpec as P

F32 = jnp.float32
BF16 = jnp.bfloat16
ANY = pl.BlockSpec(memory_space=pl.ANY)
HBM = pl.BlockSpec(memory_space=pltpu.HBM)
SMEM = pl.BlockSpec(memory_space=pltpu.SMEM)
VMEM = pl.BlockSpec(memory_space=pltpu.VMEM)
MIB = 1024 * 1024


def slot_places(block_ids, experts):
    tokens = block_ids.shape[0]
    named = jnp.sum(
        (block_ids[:, :, None] == jnp.arange(experts, dtype=jnp.int32)).astype(BF16), axis=1
    )
    row = lax.broadcasted_iota(jnp.int32, (tokens, tokens), 0)
    column = lax.broadcasted_iota(jnp.int32, (tokens, tokens), 1)
    before = (column < row).astype(BF16)
    earlier = jnp.einsum("se,ts->et", named, before, preferred_element_type=F32)
    return jnp.where(named.T > 0, earlier.astype(jnp.int32), -1)


def slot_onehot(places, first, count):
    experts, tokens = places.shape
    slot = first + jnp.arange(count, dtype=jnp.int32)
    onehot = (places[:, None, :] == slot[None, :, None]).astype(BF16)
    return onehot.reshape(experts * count, tokens)


def chip_step(value, step):
    size = lax.axis_size("local")
    chips = size // 2
    pairs = []
    for y in range(chips):
        pairs.append((2 * y, 2 * ((y + step) % chips)))
        pairs.append((2 * y + 1, 2 * ((y - step) % chips) + 1))
    return lax.ppermute(value, "local", pairs)


def core_swap(value):
    return lax.ppermute(value, "local", [(i, i ^ 1) for i in range(lax.axis_size("local"))])


def pin(values):
    return [pltpu.with_memory_space_constraint(value, pltpu.HBM) for value in values]


def after(value, *others):
    return lax.optimization_barrier((value, *others))[0]


def ring_gather(own, beside=(), between=()):
    back = chip_step(own, 1)
    on = chip_step(after(own, *beside), -1)
    far = chip_step(after(back, *between), 1)
    return back, on, far


def ring_order():
    size = lax.axis_size("local")
    chips = size // 2
    me = lax.axis_index("local")
    chip, core = me // 2, me % 2
    blocks = []
    for step in (0, -1, 1, 2):
        for other in (0, 1):
            from_core = (core + other) % 2
            moved = step * (1 - 2 * from_core)
            blocks.append(2 * ((chip + moved + chips) % chips) + from_core)
    return jnp.stack(blocks).astype(jnp.int32)


def piece_copies(pieces, buffer, sem):
    return [pltpu.make_async_copy(pieces[j], buffer.at[j], sem.at[j]) for j in range(8)]


def wait_for(ref, sem):
    pltpu.make_async_copy(ref, ref, sem).wait()


def finish(outs, sem):
    def step(j, carry):
        wait_for(outs.at[j], sem.at[j])
        return carry

    lax.fori_loop(0, outs.shape[0], step, 0)


def cost(rows, depth, columns, moved):
    return pl.CostEstimate(
        flops=2 * rows * depth * columns, bytes_accessed=moved, transcendentals=0
    )


def params(mib):
    return pltpu.CompilerParams(vmem_limit_bytes=mib * MIB)


def prepare_kernel(order, gate_a, gate_b, up_a, up_b, down_a, down_b, w_gu, own_t, send_t, w_dn):
    del order
    hidden = gate_a.shape[1]
    for i, (gate, up, down, turned) in enumerate(
        ((gate_a, up_a, down_a, own_t), (gate_b, up_b, down_b, send_t))
    ):
        w_gu[i, :, :hidden] = gate[...]
        w_gu[i, :, hidden:] = up[...]
        turned[0, :hidden, :] = gate[...].T
        turned[0, hidden:, :] = up[...].T
        w_dn[i] = down[...].T


def prepare_call(order, w_gate, w_up, w_down):
    depth, hidden = w_gate.shape
    width = depth // 8

    def rows(core):
        return pl.BlockSpec((width, hidden), lambda d, order: (order[2 * d + core], 0))

    def columns(core):
        return pl.BlockSpec((hidden, width), lambda d, order: (0, order[2 * d + core]))

    def out(count, *shape):
        return pl.BlockSpec((count, *shape), lambda d, order: (d, 0, 0))

    turned = pltpu.HBM((4, 2 * hidden, width), BF16)
    return pl.pallas_call(
        prepare_kernel,
        out_shape=(
            pltpu.HBM((8, width, 2 * hidden), BF16),
            turned,
            turned,
            pltpu.HBM((8, width, hidden), BF16),
        ),
        grid_spec=pltpu.PrefetchScalarGridSpec(
            num_scalar_prefetch=1,
            grid=(4,),
            in_specs=[rows(0), rows(1), rows(0), rows(1), columns(0), columns(1)],
            out_specs=(
                out(2, width, 2 * hidden),
                out(1, 2 * hidden, width),
                out(1, 2 * hidden, width),
                out(2, width, hidden),
            ),
        ),
        compiler_params=params(14),
        cost_estimate=cost(depth, hidden, 768, depth * hidden * 16),
        name="prepare",
    )(order, *pin((w_gate, w_gate, w_up, w_up, w_down, w_down)))


def gate_up_kernel(*refs):
    pieces, weights = refs[:8], refs[8]
    active, factors, rows_in, w_gu, acc, row_sem, w_sem = refs[9:]
    hidden = active.shape[1]
    for j in range(8):
        pltpu.make_async_copy(weights.at[j], w_gu.at[j], w_sem.at[j]).start()
    for copy in piece_copies(pieces, rows_in, row_sem):
        copy.start()
    acc[...] = jnp.zeros_like(acc)

    def step(j, carry):
        wait_for(w_gu.at[j], w_sem.at[j])
        wait_for(rows_in.at[j], row_sem.at[j])
        acc[...] += jnp.dot(rows_in[j], w_gu[j], preferred_element_type=F32)
        return carry

    lax.fori_loop(0, 8, step, 0)
    gate_pre = acc[:, :hidden]
    up_pre = acc[:, hidden:]
    sigmoid_gate = jax.nn.sigmoid(gate_pre)
    swish_gate = gate_pre * sigmoid_gate
    active[...] = (swish_gate * up_pre).astype(BF16)
    factors[:, :hidden] = up_pre * sigmoid_gate * (1.0 + gate_pre * (1.0 - sigmoid_gate))
    factors[:, hidden:] = swish_gate


def gate_up_call(pieces, w_gu):
    rows, width = pieces[0].shape
    both = w_gu.shape[2]
    hidden = both // 2
    dma = pltpu.SemaphoreType.DMA((8,))
    return pl.pallas_call(
        gate_up_kernel,
        out_shape=(
            jax.ShapeDtypeStruct((rows, hidden), BF16),
            jax.ShapeDtypeStruct((rows, both), F32),
        ),
        in_specs=[HBM] * 9,
        out_specs=(VMEM, VMEM),
        scratch_shapes=[
            pltpu.VMEM((8, rows, width), BF16),
            pltpu.VMEM((8, width, both), BF16),
            pltpu.VMEM((rows, both), F32),
            dma,
            dma,
        ],
        compiler_params=params(16),
        cost_estimate=cost(rows, 8 * width, both, 8 * width * (rows + both) * 2),
        name="gate_up",
    )(*pin((*pieces, w_gu)))


def add_hidden(first, pieces, own_w, other_w, total, w_dn, own_sem, other_sem):
    count = len(pieces)
    hidden = own_w.shape[2]
    for j in range(count):
        own = w_dn.at[j, :, pl.ds(0, hidden)]
        other = w_dn.at[j, :, pl.ds(hidden, hidden)]
        pltpu.make_async_copy(own_w.at[first + j], own, own_sem.at[j]).start()
        pltpu.make_async_copy(other_w.at[(first + j) ^ 1], other, other_sem.at[j]).start()
    for j in range(count):
        wait_for(own_w.at[0], own_sem.at[j])
        wait_for(other_w.at[0], other_sem.at[j])
        total[...] += jnp.dot(pieces[j][...], w_dn[j], preferred_element_type=F32)


def add_hidden_copied(first, pieces, own_w, other_w, total, rows_grad, w_dn, row_sem, own_sem, other_sem):
    count = len(pieces)
    hidden = own_w.shape[2]
    for j in range(count):
        own = w_dn.at[j, :, pl.ds(0, hidden)]
        other = w_dn.at[j, :, pl.ds(hidden, hidden)]
        pltpu.make_async_copy(own_w.at[first + j], own, own_sem.at[j]).start()
        pltpu.make_async_copy(other_w.at[(first + j) ^ 1], other, other_sem.at[j]).start()
        pltpu.make_async_copy(pieces[j], rows_grad.at[j], row_sem.at[j]).start()

    def step(j, carry):
        wait_for(own_w.at[0], own_sem.at[j])
        wait_for(other_w.at[0], other_sem.at[j])
        wait_for(rows_grad.at[j], row_sem.at[j])
        total[...] += jnp.dot(rows_grad[j], w_dn[j], preferred_element_type=F32)
        return carry

    lax.fori_loop(0, count, step, 0)


def hidden_start_kernel(count, *refs):
    total = refs[count + 2]
    total[...] = jnp.zeros_like(total)
    add_hidden_copied(0, refs[:count], *refs[count : count + 3], *refs[count + 3 :])


def hidden_start_call(pieces, own_w, other_w):
    rows, width = pieces[0].shape
    both, count = 2 * own_w.shape[2], len(pieces)
    dma = pltpu.SemaphoreType.DMA((count,))
    return pl.pallas_call(
        functools.partial(hidden_start_kernel, count),
        out_shape=jax.ShapeDtypeStruct((rows, both), F32),
        in_specs=[ANY] * count + [HBM] * 2,
        out_specs=VMEM,
        scratch_shapes=[
            pltpu.VMEM((count, rows, width), BF16),
            pltpu.VMEM((count, width, both), BF16),
            dma,
            dma,
            dma,
        ],
        compiler_params=params(16),
        cost_estimate=cost(rows, count * width, both, count * width * (rows + both) * 2),
        name="hidden_start",
    )(*pieces, *pin((own_w, other_w)))


def start_weights(own_w, other_w, block, buffer, own_sem, other_sem):
    both = own_w.shape[1]
    pltpu.make_async_copy(own_w.at[block], buffer.at[pl.ds(0, both), :], own_sem).start()
    pltpu.make_async_copy(other_w.at[block], buffer.at[pl.ds(both, both), :], other_sem).start()


def hidden_end_kernel(first, count, block, *refs):
    pieces = refs[:count]
    own_dn, other_dn, own_w, other_w, before, own_factors, other_factors = refs[count : count + 7]
    grads, out = refs[count + 7 : count + 9]
    total, w_dn, w_gu, result, own_sem, other_sem, w_sem, out_sem = refs[count + 9 :]
    start_weights(own_w, other_w, block, w_gu, w_sem.at[0], w_sem.at[1])
    total[...] = before[...]
    add_hidden(first, pieces, own_dn, other_dn, total, w_dn, own_sem, other_sem)
    hidden = own_dn.shape[2]
    for core, factors in enumerate((own_factors, other_factors)):
        hidden_grad = total[:, core * hidden : (core + 1) * hidden]
        at = 2 * core * hidden
        grads[:, at : at + hidden] = (hidden_grad * factors[:, :hidden]).astype(BF16)
        grads[:, at + hidden : at + 2 * hidden] = (hidden_grad * factors[:, hidden:]).astype(BF16)
    wait_for(own_w.at[0], w_sem.at[0])
    wait_for(other_w.at[0], w_sem.at[1])
    result[...] = jnp.dot(grads[...], w_gu[...], preferred_element_type=F32).astype(BF16)
    copy = pltpu.make_async_copy(result, out, out_sem)
    copy.start()
    copy.wait()


def hidden_end_call(pieces, own_dn, other_dn, own_w, other_w, before, factors, others, block):
    rows, width = pieces[0].shape
    both, count = 2 * own_dn.shape[2], len(pieces)
    dma = pltpu.SemaphoreType.DMA
    return pl.pallas_call(
        functools.partial(hidden_end_kernel, own_dn.shape[0] - count, count, block),
        out_shape=(
            jax.ShapeDtypeStruct((rows, 2 * both), BF16),
            jax.ShapeDtypeStruct((rows, width), BF16),
        ),
        in_specs=[VMEM] * count + [HBM] * 4 + [VMEM] * 3,
        out_specs=(VMEM, ANY),
        scratch_shapes=[
            pltpu.VMEM((rows, both), F32),
            pltpu.VMEM((count, width, both), BF16),
            pltpu.VMEM((2 * both, width), BF16),
            pltpu.VMEM((rows, width), BF16),
            dma((count,)),
            dma((count,)),
            dma((2,)),
            dma,
        ],
        compiler_params=params(20),
        cost_estimate=cost(rows, (count + 2) * width, both, count * width * (rows + both) * 2),
        name="hidden_end",
    )(*pieces, *pin((own_dn, other_dn, own_w, other_w)), before, factors, others)


def partial_kernel(blocks, *refs):
    count = len(blocks)
    grads, own_w, other_w = refs[:3]
    outs = refs[3 : 3 + count]
    w_gu, result, own_sem, other_sem, out_sem = refs[3 + count :]
    for i, j in enumerate(blocks):
        start_weights(own_w, other_w, j, w_gu.at[i], own_sem.at[i], other_sem.at[i])
    for i in range(count):
        wait_for(own_w.at[0], own_sem.at[i])
        wait_for(other_w.at[0], other_sem.at[i])
        result[i] = jnp.dot(grads[...], w_gu[i], preferred_element_type=F32).astype(BF16)
        pltpu.make_async_copy(result.at[i], outs[i], out_sem.at[i]).start()
    finish(result, out_sem)


def partial_call(grads, own_w, other_w, blocks):
    both, width = own_w.shape[1:]
    rows, count = grads.shape[0], len(blocks)
    dma = pltpu.SemaphoreType.DMA((count,))
    return pl.pallas_call(
        functools.partial(partial_kernel, blocks),
        out_shape=[jax.ShapeDtypeStruct((rows, width), BF16)] * count,
        in_specs=[VMEM, HBM, HBM],
        out_specs=[ANY] * count,
        scratch_shapes=[
            pltpu.VMEM((count, 2 * both, width), BF16),
            pltpu.VMEM((count, rows, width), BF16),
            dma,
            dma,
            dma,
        ],
        compiler_params=params(14),
        cost_estimate=cost(
            rows, 2 * both, count * width, count * 2 * width * (rows + 2 * both) * 2
        ),
        name="partial",
    )(grads, *pin((own_w, other_w)))


def down_total_kernel(order, *refs):
    pieces = refs[:8]
    active, grad_down, rows_grad, out, row_sem, out_sem = refs[8:]
    width = out.shape[2]
    for copy in piece_copies(pieces, rows_grad, row_sem):
        copy.start()

    def step(j, carry):
        wait_for(rows_grad.at[j], row_sem.at[j])
        out[j] = jnp.dot(active[...], rows_grad[j], preferred_element_type=F32).astype(BF16)
        at = pl.ds(pl.multiple_of(order[j] * width, width), width)
        pltpu.make_async_copy(out.at[j], grad_down.at[:, at], out_sem.at[j]).start()
        return carry

    lax.fori_loop(0, 8, step, 0)
    finish(out, out_sem)


def down_total_call(order, pieces, active):
    width = pieces[0].shape[1]
    hidden, rows = active.shape
    dma = pltpu.SemaphoreType.DMA((8,))
    return pl.pallas_call(
        down_total_kernel,
        out_shape=jax.ShapeDtypeStruct((hidden, 8 * width), BF16),
        in_specs=[SMEM] + [HBM] * 8 + [VMEM],
        out_specs=HBM,
        scratch_shapes=[
            pltpu.VMEM((8, rows, width), BF16),
            pltpu.VMEM((8, hidden, width), BF16),
            dma,
            dma,
        ],
        compiler_params=params(12),
        cost_estimate=cost(rows, 8 * width, hidden, 8 * width * (rows + hidden) * 2),
        name="down_total",
    )(order, *pin(pieces), active)


def gate_up_total_kernel(order, *refs):
    pieces = refs[:8]
    grads, grad_gate, grad_up, rows_in, out_gate, out_up, row_sem, gate_sem, up_sem = refs[8:]
    width, hidden = out_gate.shape[1:]
    for copy in piece_copies(pieces, rows_in, row_sem):
        copy.start()

    def step(j, carry):
        wait_for(rows_in.at[j], row_sem.at[j])
        both = lax.dot_general(
            rows_in[j],
            grads[:, : 2 * hidden],
            (((0,), (0,)), ((), ())),
            preferred_element_type=F32,
        )
        out_gate[j] = both[:, :hidden].astype(BF16)
        out_up[j] = both[:, hidden:].astype(BF16)
        at = pl.ds(pl.multiple_of(order[j] * width, width), width)
        pltpu.make_async_copy(out_gate.at[j], grad_gate.at[at, :], gate_sem.at[j]).start()
        pltpu.make_async_copy(out_up.at[j], grad_up.at[at, :], up_sem.at[j]).start()
        return carry

    lax.fori_loop(0, 8, step, 0)
    finish(out_gate, gate_sem)
    finish(out_up, up_sem)


def gate_up_total_call(order, pieces, grads):
    width = pieces[0].shape[1]
    rows, both = grads.shape[0], grads.shape[1] // 2
    hidden = both // 2
    dma = pltpu.SemaphoreType.DMA((8,))
    total = jax.ShapeDtypeStruct((8 * width, hidden), BF16)
    return pl.pallas_call(
        gate_up_total_kernel,
        out_shape=(total, total),
        in_specs=[SMEM] + [HBM] * 8 + [VMEM],
        out_specs=(HBM, HBM),
        scratch_shapes=[
            pltpu.VMEM((8, rows, width), BF16),
            pltpu.VMEM((8, width, hidden), BF16),
            pltpu.VMEM((8, width, hidden), BF16),
            dma,
            dma,
            dma,
        ],
        compiler_params=params(16),
        cost_estimate=cost(rows, 8 * width, both, 8 * width * (rows + both) * 2),
        name="gate_up_total",
    )(order, *pin(pieces), grads)


def body(tokens_in, grad_out, expert_ids, w_gate, w_up, w_down):
    experts = lax.axis_size("node")
    token_count, topk = expert_ids.shape
    capacity = token_count * topk * 3 // (2 * experts)
    places = slot_places(expert_ids, experts)
    onehot = slot_onehot(places, 0, capacity)

    def packed(table):
        return jnp.dot(onehot, table, preferred_element_type=F32).astype(BF16)

    def exchange(value):
        return lax.all_to_all(value, "node", split_axis=0, concat_axis=0, tiled=True)

    packed_grad = packed(grad_out)
    order = after(ring_order(), packed_grad)
    w_gu, own_w, send_w, w_dn = prepare_call(order, w_gate[0], w_up[0], w_down[0])
    arrived_in = after(exchange(packed(tokens_in)), w_gu)
    arrived_grad = exchange(after(packed_grad, arrived_in))
    back, on, far = ring_gather(arrived_in)
    pieces_in = (arrived_in, core_swap(arrived_in), back, core_swap(back), on, core_swap(on))
    pieces_in = (*pieces_in, far, core_swap(far))
    other_w = core_swap(after(send_w, back))
    other_dn = core_swap(after(w_dn, back))
    active, factors = gate_up_call(pieces_in, w_gu)
    back, on, far = ring_gather(after(arrived_grad, far))
    others = core_swap(factors)
    near = (arrived_grad, core_swap(arrived_grad), back, core_swap(back), on, core_swap(on))
    before = hidden_start_call(near, w_dn, other_dn)
    far = after(far, before, active)
    late = (far, core_swap(far))
    pieces_grad = (*near, *late)
    grads, far = hidden_end_call(
        late, w_dn, other_dn, own_w, other_w, before, factors, others, 3
    )
    far = chip_step(far, 1)
    back, own, on = partial_call(grads, own_w, other_w, (1, 0, 2))
    back = chip_step(back, -1)
    joined = on.astype(F32) + far.astype(F32)
    on = chip_step(joined.astype(BF16), 1)
    total = (own.astype(F32) + back.astype(F32) + on.astype(F32)).astype(BF16)
    down_total = down_total_call(order, pieces_grad, active.T)
    gate_total, up_total = gate_up_total_call(order, pieces_in, grads)
    returned = exchange(total)
    grad_in = jnp.einsum("st,sd->td", onehot, returned, preferred_element_type=F32)
    return (grad_in.astype(BF16), gate_total[None], up_total[None], down_total[None])


def solution(mesh):
    placed = (
        P("node", "local"),
        P("node", "local"),
        P("node", None),
        P("node", None, "local"),
        P("node", None, "local"),
        P("node", "local", None),
    )
    return jax.shard_map(
        body,
        mesh=mesh,
        in_specs=placed,
        out_specs=(
            P("node", "local"),
            P("node", None, "local"),
            P("node", None, "local"),
            P("node", "local", None),
        ),
        check_vma=False,
    )
```

```python
import functools

import jax
import jax.numpy as jnp
from jax import lax
from jax.experimental import pallas as pl
from jax.experimental.pallas import tpu as pltpu
from jax.sharding import PartitionSpec as P

F32 = jnp.float32
BF16 = jnp.bfloat16
ANY = pl.BlockSpec(memory_space=pl.ANY)
HBM = pl.BlockSpec(memory_space=pltpu.HBM)
SMEM = pl.BlockSpec(memory_space=pltpu.SMEM)
VMEM = pl.BlockSpec(memory_space=pltpu.VMEM)
MIB = 1024 * 1024


def slot_places(block_ids, experts):
    tokens = block_ids.shape[0]
    named = jnp.sum(
        (block_ids[:, :, None] == jnp.arange(experts, dtype=jnp.int32)).astype(BF16), axis=1
    )
    row = lax.broadcasted_iota(jnp.int32, (tokens, tokens), 0)
    column = lax.broadcasted_iota(jnp.int32, (tokens, tokens), 1)
    before = (column < row).astype(BF16)
    earlier = jnp.einsum("se,ts->et", named, before, preferred_element_type=F32)
    return jnp.where(named.T > 0, earlier.astype(jnp.int32), -1)


def slot_onehot(places, first, count):
    experts, tokens = places.shape
    slot = first + jnp.arange(count, dtype=jnp.int32)
    onehot = (places[:, None, :] == slot[None, :, None]).astype(BF16)
    return onehot.reshape(experts * count, tokens)


def chip_step(value, step):
    size = lax.axis_size("local")
    chips = size // 2
    pairs = []
    for y in range(chips):
        pairs.append((2 * y, 2 * ((y + step) % chips)))
        pairs.append((2 * y + 1, 2 * ((y - step) % chips) + 1))
    return lax.ppermute(value, "local", pairs)


def core_swap(value):
    return lax.ppermute(value, "local", [(i, i ^ 1) for i in range(lax.axis_size("local"))])


def pin(values):
    return [pltpu.with_memory_space_constraint(value, pltpu.HBM) for value in values]


def after(value, *others):
    return lax.optimization_barrier((value, *others))[0]


def ring_gather(own, beside=(), between=()):
    back = chip_step(own, 1)
    on = chip_step(after(own, *beside), -1)
    far = chip_step(after(back, *between), 1)
    return back, on, far


def ring_order():
    size = lax.axis_size("local")
    chips = size // 2
    me = lax.axis_index("local")
    chip, core = me // 2, me % 2
    blocks = []
    for step in (0, -1, 1, 2):
        for other in (0, 1):
            from_core = (core + other) % 2
            moved = step * (1 - 2 * from_core)
            blocks.append(2 * ((chip + moved + chips) % chips) + from_core)
    return jnp.stack(blocks).astype(jnp.int32)


def piece_copies(pieces, buffer, sem):
    return [pltpu.make_async_copy(pieces[j], buffer.at[j], sem.at[j]) for j in range(8)]


def wait_for(ref, sem):
    pltpu.make_async_copy(ref, ref, sem).wait()


def finish(outs, sem):
    def step(j, carry):
        wait_for(outs.at[j], sem.at[j])
        return carry

    lax.fori_loop(0, outs.shape[0], step, 0)


def cost(rows, depth, columns, moved):
    return pl.CostEstimate(
        flops=2 * rows * depth * columns, bytes_accessed=moved, transcendentals=0
    )


def params(mib):
    return pltpu.CompilerParams(vmem_limit_bytes=mib * MIB)


def prepare_kernel(order, gate_a, gate_b, up_a, up_b, down_a, down_b, w_gu, own_t, send_t, w_dn):
    del order
    hidden = gate_a.shape[1]
    for i, (gate, up, down, turned) in enumerate(
        ((gate_a, up_a, down_a, own_t), (gate_b, up_b, down_b, send_t))
    ):
        w_gu[i, :, :hidden] = gate[...]
        w_gu[i, :, hidden:] = up[...]
        turned[0, :hidden, :] = gate[...].T
        turned[0, hidden:, :] = up[...].T
        w_dn[i] = down[...].T


def prepare_call(order, w_gate, w_up, w_down):
    depth, hidden = w_gate.shape
    width = depth // 8

    def rows(core):
        return pl.BlockSpec((width, hidden), lambda d, order: (order[2 * d + core], 0))

    def columns(core):
        return pl.BlockSpec((hidden, width), lambda d, order: (0, order[2 * d + core]))

    def out(count, *shape):
        return pl.BlockSpec((count, *shape), lambda d, order: (d, 0, 0))

    turned = pltpu.HBM((4, 2 * hidden, width), BF16)
    return pl.pallas_call(
        prepare_kernel,
        out_shape=(
            pltpu.HBM((8, width, 2 * hidden), BF16),
            turned,
            turned,
            pltpu.HBM((8, width, hidden), BF16),
        ),
        grid_spec=pltpu.PrefetchScalarGridSpec(
            num_scalar_prefetch=1,
            grid=(4,),
            in_specs=[rows(0), rows(1), rows(0), rows(1), columns(0), columns(1)],
            out_specs=(
                out(2, width, 2 * hidden),
                out(1, 2 * hidden, width),
                out(1, 2 * hidden, width),
                out(2, width, hidden),
            ),
        ),
        compiler_params=params(14),
        cost_estimate=cost(depth, hidden, 768, depth * hidden * 16),
        name="prepare",
    )(order, *pin((w_gate, w_gate, w_up, w_up, w_down, w_down)))


def gate_up_kernel(*refs):
    pieces, weights = refs[:8], refs[8]
    active, factors, rows_in, w_gu, acc, row_sem, w_sem = refs[9:]
    hidden = active.shape[1]
    for j in range(8):
        pltpu.make_async_copy(weights.at[j], w_gu.at[j], w_sem.at[j]).start()
    for copy in piece_copies(pieces, rows_in, row_sem):
        copy.start()
    acc[...] = jnp.zeros_like(acc)

    def step(j, carry):
        wait_for(w_gu.at[j], w_sem.at[j])
        wait_for(rows_in.at[j], row_sem.at[j])
        acc[...] += jnp.dot(rows_in[j], w_gu[j], preferred_element_type=F32)
        return carry

    lax.fori_loop(0, 8, step, 0)
    gate_pre = acc[:, :hidden]
    up_pre = acc[:, hidden:]
    sigmoid_gate = jax.nn.sigmoid(gate_pre)
    swish_gate = gate_pre * sigmoid_gate
    active[...] = (swish_gate * up_pre).astype(BF16)
    factors[:, :hidden] = up_pre * sigmoid_gate * (1.0 + gate_pre * (1.0 - sigmoid_gate))
    factors[:, hidden:] = swish_gate


def gate_up_call(pieces, w_gu):
    rows, width = pieces[0].shape
    both = w_gu.shape[2]
    hidden = both // 2
    dma = pltpu.SemaphoreType.DMA((8,))
    return pl.pallas_call(
        gate_up_kernel,
        out_shape=(
            jax.ShapeDtypeStruct((rows, hidden), BF16),
            jax.ShapeDtypeStruct((rows, both), F32),
        ),
        in_specs=[HBM] * 9,
        out_specs=(VMEM, VMEM),
        scratch_shapes=[
            pltpu.VMEM((8, rows, width), BF16),
            pltpu.VMEM((8, width, both), BF16),
            pltpu.VMEM((rows, both), F32),
            dma,
            dma,
        ],
        compiler_params=params(16),
        cost_estimate=cost(rows, 8 * width, both, 8 * width * (rows + both) * 2),
        name="gate_up",
    )(*pin((*pieces, w_gu)))


def add_hidden(first, pieces, own_w, other_w, total, w_dn, own_sem, other_sem):
    count = len(pieces)
    hidden = own_w.shape[2]
    for j in range(count):
        own = w_dn.at[j, :, pl.ds(0, hidden)]
        other = w_dn.at[j, :, pl.ds(hidden, hidden)]
        pltpu.make_async_copy(own_w.at[first + j], own, own_sem.at[j]).start()
        pltpu.make_async_copy(other_w.at[(first + j) ^ 1], other, other_sem.at[j]).start()
    for j in range(count):
        wait_for(own_w.at[0], own_sem.at[j])
        wait_for(other_w.at[0], other_sem.at[j])
        total[...] += jnp.dot(pieces[j][...], w_dn[j], preferred_element_type=F32)


def add_hidden_copied(first, pieces, own_w, other_w, total, rows_grad, w_dn, row_sem, own_sem, other_sem):
    count = len(pieces)
    hidden = own_w.shape[2]
    for j in range(count):
        own = w_dn.at[j, :, pl.ds(0, hidden)]
        other = w_dn.at[j, :, pl.ds(hidden, hidden)]
        pltpu.make_async_copy(own_w.at[first + j], own, own_sem.at[j]).start()
        pltpu.make_async_copy(other_w.at[(first + j) ^ 1], other, other_sem.at[j]).start()
        pltpu.make_async_copy(pieces[j], rows_grad.at[j], row_sem.at[j]).start()

    def step(j, carry):
        wait_for(own_w.at[0], own_sem.at[j])
        wait_for(other_w.at[0], other_sem.at[j])
        wait_for(rows_grad.at[j], row_sem.at[j])
        total[...] += jnp.dot(rows_grad[j], w_dn[j], preferred_element_type=F32)
        return carry

    lax.fori_loop(0, count, step, 0)


def hidden_start_kernel(count, *refs):
    total = refs[count + 2]
    total[...] = jnp.zeros_like(total)
    add_hidden_copied(0, refs[:count], *refs[count : count + 3], *refs[count + 3 :])


def hidden_start_call(pieces, own_w, other_w):
    rows, width = pieces[0].shape
    both, count = 2 * own_w.shape[2], len(pieces)
    dma = pltpu.SemaphoreType.DMA((count,))
    return pl.pallas_call(
        functools.partial(hidden_start_kernel, count),
        out_shape=jax.ShapeDtypeStruct((rows, both), F32),
        in_specs=[ANY] * count + [HBM] * 2,
        out_specs=VMEM,
        scratch_shapes=[
            pltpu.VMEM((count, rows, width), BF16),
            pltpu.VMEM((count, width, both), BF16),
            dma,
            dma,
            dma,
        ],
        compiler_params=params(16),
        cost_estimate=cost(rows, count * width, both, count * width * (rows + both) * 2),
        name="hidden_start",
    )(*pieces, *pin((own_w, other_w)))


def start_weights(own_w, other_w, block, buffer, own_sem, other_sem):
    both = own_w.shape[1]
    pltpu.make_async_copy(own_w.at[block], buffer.at[pl.ds(0, both), :], own_sem).start()
    pltpu.make_async_copy(other_w.at[block], buffer.at[pl.ds(both, both), :], other_sem).start()


def hidden_end_kernel(first, count, block, *refs):
    pieces = refs[:count]
    own_dn, other_dn, own_w, other_w, before, own_factors, other_factors = refs[count : count + 7]
    grads, out = refs[count + 7 : count + 9]
    total, w_dn, w_gu, own_sem, other_sem, w_sem = refs[count + 9 :]
    start_weights(own_w, other_w, block, w_gu, w_sem.at[0], w_sem.at[1])
    total[...] = before[...]
    add_hidden(first, pieces, own_dn, other_dn, total, w_dn, own_sem, other_sem)
    hidden = own_dn.shape[2]
    for core, factors in enumerate((own_factors, other_factors)):
        hidden_grad = total[:, core * hidden : (core + 1) * hidden]
        at = 2 * core * hidden
        grads[:, at : at + hidden] = (hidden_grad * factors[:, :hidden]).astype(BF16)
        grads[:, at + hidden : at + 2 * hidden] = (hidden_grad * factors[:, hidden:]).astype(BF16)
    wait_for(own_w.at[0], w_sem.at[0])
    wait_for(other_w.at[0], w_sem.at[1])
    out[...] = jnp.dot(grads[...], w_gu[...], preferred_element_type=F32).astype(BF16)


def hidden_end_call(pieces, own_dn, other_dn, own_w, other_w, before, factors, others, block):
    rows, width = pieces[0].shape
    both, count = 2 * own_dn.shape[2], len(pieces)
    dma = pltpu.SemaphoreType.DMA
    return pl.pallas_call(
        functools.partial(hidden_end_kernel, own_dn.shape[0] - count, count, block),
        out_shape=(
            jax.ShapeDtypeStruct((rows, 2 * both), BF16),
            jax.ShapeDtypeStruct((rows, width), BF16),
        ),
        in_specs=[VMEM] * count + [HBM] * 4 + [VMEM] * 3,
        out_specs=(VMEM, VMEM),
        scratch_shapes=[
            pltpu.VMEM((rows, both), F32),
            pltpu.VMEM((count, width, both), BF16),
            pltpu.VMEM((2 * both, width), BF16),
            dma((count,)),
            dma((count,)),
            dma((2,)),
        ],
        compiler_params=params(20),
        cost_estimate=cost(rows, (count + 2) * width, both, count * width * (rows + both) * 2),
        name="hidden_end",
    )(*pieces, *pin((own_dn, other_dn, own_w, other_w)), before, factors, others)


def partial_kernel(blocks, *refs):
    count = len(blocks)
    grads, own_w, other_w = refs[:3]
    outs = refs[3 : 3 + count]
    w_gu, own_sem, other_sem = refs[3 + count :]
    for i, j in enumerate(blocks):
        start_weights(own_w, other_w, j, w_gu.at[i], own_sem.at[i], other_sem.at[i])
    for i in range(count):
        wait_for(own_w.at[0], own_sem.at[i])
        wait_for(other_w.at[0], other_sem.at[i])
        outs[i][...] = jnp.dot(grads[...], w_gu[i], preferred_element_type=F32).astype(BF16)


def partial_call(grads, own_w, other_w, blocks):
    both, width = own_w.shape[1:]
    rows, count = grads.shape[0], len(blocks)
    dma = pltpu.SemaphoreType.DMA((count,))
    return pl.pallas_call(
        functools.partial(partial_kernel, blocks),
        out_shape=[jax.ShapeDtypeStruct((rows, width), BF16)] * count,
        in_specs=[VMEM, HBM, HBM],
        out_specs=[VMEM] * count,
        scratch_shapes=[
            pltpu.VMEM((count, 2 * both, width), BF16),
            dma,
            dma,
        ],
        compiler_params=params(14),
        cost_estimate=cost(
            rows, 2 * both, count * width, count * 2 * width * (rows + 2 * both) * 2
        ),
        name="partial",
    )(grads, *pin((own_w, other_w)))


def down_total_kernel(order, *refs):
    pieces = refs[:8]
    active, grad_down, rows_grad, out, row_sem, out_sem = refs[8:]
    width = out.shape[2]
    for copy in piece_copies(pieces, rows_grad, row_sem):
        copy.start()

    def step(j, carry):
        wait_for(rows_grad.at[j], row_sem.at[j])
        out[j] = jnp.dot(active[...], rows_grad[j], preferred_element_type=F32).astype(BF16)
        at = pl.ds(pl.multiple_of(order[j] * width, width), width)
        pltpu.make_async_copy(out.at[j], grad_down.at[:, at], out_sem.at[j]).start()
        return carry

    lax.fori_loop(0, 8, step, 0)
    finish(out, out_sem)


def down_total_call(order, pieces, active):
    width = pieces[0].shape[1]
    hidden, rows = active.shape
    dma = pltpu.SemaphoreType.DMA((8,))
    return pl.pallas_call(
        down_total_kernel,
        out_shape=jax.ShapeDtypeStruct((hidden, 8 * width), BF16),
        in_specs=[SMEM] + [HBM] * 8 + [VMEM],
        out_specs=HBM,
        scratch_shapes=[
            pltpu.VMEM((8, rows, width), BF16),
            pltpu.VMEM((8, hidden, width), BF16),
            dma,
            dma,
        ],
        compiler_params=params(12),
        cost_estimate=cost(rows, 8 * width, hidden, 8 * width * (rows + hidden) * 2),
        name="down_total",
    )(order, *pin(pieces), active)


def gate_up_total_kernel(order, *refs):
    pieces = refs[:8]
    grads, grad_gate, grad_up, rows_in, out_gate, out_up, row_sem, gate_sem, up_sem = refs[8:]
    width, hidden = out_gate.shape[1:]
    for copy in piece_copies(pieces, rows_in, row_sem):
        copy.start()

    def step(j, carry):
        wait_for(rows_in.at[j], row_sem.at[j])
        both = lax.dot_general(
            rows_in[j],
            grads[:, : 2 * hidden],
            (((0,), (0,)), ((), ())),
            preferred_element_type=F32,
        )
        out_gate[j] = both[:, :hidden].astype(BF16)
        out_up[j] = both[:, hidden:].astype(BF16)
        at = pl.ds(pl.multiple_of(order[j] * width, width), width)
        pltpu.make_async_copy(out_gate.at[j], grad_gate.at[at, :], gate_sem.at[j]).start()
        pltpu.make_async_copy(out_up.at[j], grad_up.at[at, :], up_sem.at[j]).start()
        return carry

    lax.fori_loop(0, 8, step, 0)
    finish(out_gate, gate_sem)
    finish(out_up, up_sem)


def gate_up_total_call(order, pieces, grads):
    width = pieces[0].shape[1]
    rows, both = grads.shape[0], grads.shape[1] // 2
    hidden = both // 2
    dma = pltpu.SemaphoreType.DMA((8,))
    total = jax.ShapeDtypeStruct((8 * width, hidden), BF16)
    return pl.pallas_call(
        gate_up_total_kernel,
        out_shape=(total, total),
        in_specs=[SMEM] + [HBM] * 8 + [VMEM],
        out_specs=(HBM, HBM),
        scratch_shapes=[
            pltpu.VMEM((8, rows, width), BF16),
            pltpu.VMEM((8, width, hidden), BF16),
            pltpu.VMEM((8, width, hidden), BF16),
            dma,
            dma,
            dma,
        ],
        compiler_params=params(16),
        cost_estimate=cost(rows, 8 * width, both, 8 * width * (rows + both) * 2),
        name="gate_up_total",
    )(order, *pin(pieces), grads)


def body(tokens_in, grad_out, expert_ids, w_gate, w_up, w_down):
    experts = lax.axis_size("node")
    token_count, topk = expert_ids.shape
    capacity = token_count * topk * 3 // (2 * experts)
    places = slot_places(expert_ids, experts)
    onehot = slot_onehot(places, 0, capacity)

    def packed(table):
        return jnp.dot(onehot, table, preferred_element_type=F32).astype(BF16)

    def exchange(value):
        return lax.all_to_all(value, "node", split_axis=0, concat_axis=0, tiled=True)

    packed_grad = packed(grad_out)
    order = after(ring_order(), packed_grad)
    w_gu, own_w, send_w, w_dn = prepare_call(order, w_gate[0], w_up[0], w_down[0])
    arrived_in = after(exchange(packed(tokens_in)), w_gu)
    arrived_grad = exchange(after(packed_grad, arrived_in))
    back, on, far = ring_gather(arrived_in)
    pieces_in = (arrived_in, core_swap(arrived_in), back, core_swap(back), on, core_swap(on))
    pieces_in = (*pieces_in, far, core_swap(far))
    other_w = core_swap(after(send_w, back))
    other_dn = core_swap(after(w_dn, back))
    active, factors = gate_up_call(pieces_in, w_gu)
    back, on, far = ring_gather(after(arrived_grad, far))
    others = core_swap(factors)
    near = (arrived_grad, core_swap(arrived_grad), back, core_swap(back), on, core_swap(on))
    before = hidden_start_call(near, w_dn, other_dn)
    far = after(far, before, active)
    late = (far, core_swap(far))
    pieces_grad = (*near, *late)
    grads, far = hidden_end_call(
        late, w_dn, other_dn, own_w, other_w, before, factors, others, 3
    )
    far = chip_step(far, 1)
    back, own, on = partial_call(grads, own_w, other_w, (1, 0, 2))
    back = chip_step(back, -1)
    joined = on.astype(F32) + far.astype(F32)
    on = chip_step(joined.astype(BF16), 1)
    total = (own.astype(F32) + back.astype(F32) + on.astype(F32)).astype(BF16)
    down_total = down_total_call(order, pieces_grad, active.T)
    gate_total, up_total = gate_up_total_call(order, pieces_in, grads)
    returned = exchange(total)
    grad_in = jnp.einsum("st,sd->td", onehot, returned, preferred_element_type=F32)
    return (grad_in.astype(BF16), gate_total[None], up_total[None], down_total[None])


def solution(mesh):
    placed = (
        P("node", "local"),
        P("node", "local"),
        P("node", None),
        P("node", None, "local"),
        P("node", None, "local"),
        P("node", "local", None),
    )
    return jax.shard_map(
        body,
        mesh=mesh,
        in_specs=placed,
        out_specs=(
            P("node", "local"),
            P("node", None, "local"),
            P("node", None, "local"),
            P("node", "local", None),
        ),
        check_vma=False,
    )
```
